512 devices in a mesh: row: 8 (over x, y_lo), col: 16 (over z), rep: 4 (over y_hi, core).
Axes of the slice: x: 4, y: 4 (y_hi: 2, y_lo: 2; y = y_hi * 2 + y_lo), z: 16, core: 2. Of those that a mesh axis runs over, the one named last changes fastest.
Arguments:
- layer_input: bfloat16 [2048, 12288], P('col', ('row', 'rep')), may hold values from -0.75 to 0.75
- weight: bfloat16 [12288, 24576], P(('row', 'rep'), 'col'), may hold values from -0.0546875 to 0.0546875
- gelu_input: bfloat16 [2048, 24576], P(('row', 'rep'), 'col'), may hold values from -8 to 8
- upstream: bfloat16 [2048, 24576], P(('row', 'rep'), 'col'), may hold values from -6 to 6
Outputs:
- grad_input: bfloat16 [2048, 12288], P('col', ('row', 'rep'))
- grad_weight: float32 [12288, 24576], P(('row', 'rep'), 'col')
The draws below stay inside these ranges and needn't reach their ends.
All inputs are finite; a program needn't handle non-finite values.
Results may differ from the reference program's by a relative error of at most 0.024.
Values may be sent and summed in bfloat16 or wider, within the bound.
No kernel may reach another device: no remote copies, remote signals or barrier semaphores. Data moves between devices by JAX's collectives and lax.ppermute only.
A program may use at most 64 MiB of HBM per device.

```python
import math
import jax
import jax.numpy as jnp
from jax import lax

D = 12288
FF = 24576
TOKENS = 2048
N_COL = 16


def with_spikes(array, stream_key, source, target, shards_of, factor):
    def block_of(axis_at):
        return (jnp.arange(array.shape[axis_at]) // (array.shape[axis_at] // shards_of)).reshape((-1,) + (1,) * (array.ndim - 1 - axis_at))

    near = jax.random.permutation(stream_key, shards_of)[block_of(target)]
    other_side = (block_of(target) + shards_of // 2) % shards_of
    return jnp.where((block_of(source) == near) | (block_of(source) == other_side), factor * array, array)


def steps_of(stream_key, shape, cuts, smallest, top_value):
    factor_of, own = 1.0, jax.random.fold_in(stream_key, 6)
    for position, blocks in cuts:
        heights = jnp.exp(jax.random.uniform(jax.random.fold_in(own, position), (blocks,), jnp.float32, smallest / len(cuts), top_value / len(cuts)))
        factor_of = factor_of * jnp.repeat(heights, shape[position] // blocks).reshape([-1 if axis == position else 1 for axis in range(len(shape))])
    return factor_of


def normal_values(stream_key, dims, deviation, most, pieces=(), held_as=jnp.bfloat16):
    gain = steps_of(stream_key, dims, pieces, -0.22, 0.18) if pieces else 1.0
    array = jax.random.normal(stream_key, dims, jnp.float32) * deviation * gain
    return jnp.minimum(jnp.maximum(array, -most), most).astype(held_as)


def heavy_noise(key, shape, width, limit, cuts, heavy, dtype=jnp.bfloat16):
    values = width * jax.random.normal(key, shape, jnp.float32)
    if cuts:
        values = values * steps_of(key, shape, cuts, -0.22, 0.18)
    return jnp.clip(with_spikes(values, jax.random.fold_in(key, 3), *heavy), -limit, limit).astype(dtype)


def setup_inputs(seed: int = 0) -> dict:
    arg_keys = jax.random.split(jax.random.key(seed), 5)
    return {
        "layer_input": normal_values(arg_keys[0], (TOKENS, D), 0.125, 0.75, ((0, 16), (1, 32))),
        "weight": normal_values(arg_keys[1], (D, FF), D ** -0.5, 0.0546875, ((0, 32), (1, 16))),
        "gelu_input": normal_values(arg_keys[2], (TOKENS, FF), 1.5, 8.0, ((0, 32), (1, 16))),
        "upstream": heavy_noise(arg_keys[3], (TOKENS, FF), 1.0, 6.0, ((0, 32), (1, 16)), (1, 0, 32, 2.75)),
    }


cubic_term = 0.044715

def gelu_slope(values):
    scale = math.sqrt(2.0 / math.pi)
    inner = scale * (values + cubic_term * values * values * values)
    tangent = jnp.tanh(inner)
    return 0.5 * (1.0 + tangent) + 0.5 * values * (1.0 - tangent * tangent) * scale * (1.0 + 3.0 * cubic_term * values * values)

def reference(layer_input, weight, gelu_input, upstream):
    gelu_grad = (upstream.astype(jnp.float32) * gelu_slope(gelu_input.astype(jnp.float32))).astype(jnp.bfloat16)
    block_width = FF // N_COL

    def add_block(index, total):
        start = (index * block_width).astype(jnp.int32)
        grad_block = lax.dynamic_slice_in_dim(gelu_grad, start, block_width, 1)
        weight_block = lax.dynamic_slice_in_dim(weight, start, block_width, 1)
        block_sum = lax.dot_general(grad_block, weight_block, (((1,), (1,)), ((), ())), preferred_element_type=jnp.float32).astype(jnp.bfloat16)
        return total + block_sum.astype(jnp.float32)
    summed = lax.fori_loop(0, N_COL, add_block, jnp.zeros((TOKENS, D), jnp.float32))
    grad_input = summed.astype(jnp.bfloat16)
    grad_weight = lax.dot_general(layer_input, gelu_grad, (((0,), (0,)), ((), ())), preferred_element_type=jnp.float32)
    return (grad_input, grad_weight)
```

```python
import functools
import math

import jax
import jax.numpy as jnp
import numpy as np
from jax import lax
from jax.experimental import pallas as pl
from jax.experimental.pallas import tpu as pltpu
from jax.sharding import PartitionSpec as P

cubic_term = 0.044715
plane = ("row", "rep")
ring = ("col", "rep")


def gelu_slope(values):
    scale = math.sqrt(2.0 / math.pi)
    inner = scale * (values + cubic_term * values * values * values)
    tangent = jnp.tanh(inner)
    return 0.5 * (1.0 + tangent) + 0.5 * values * (1.0 - tangent * tangent) * scale * (
        1.0 + 3.0 * cubic_term * values * values
    )


def index(x, y, core):
    return ((x * 2 + y % 2) * 2 + y // 2) * 2 + core


y_order = (0, 2, 1, 3)
along_x = [[[index(x, y, core) for x in range(4)] for y in y_order] for core in range(2)]
along_y = [[[index(x, y, core) for y in y_order] for x in range(4)] for core in range(2)]


early_steps = (7, 5, 3, 1, 8, -7, -5, -3, -1)
late_steps = (6, 4, 2, 0, -6, -4, -2)


def order_of(steps):
    table = np.zeros((32, len(steps)), np.int32)
    for z in range(16):
        for i, step in enumerate(steps):
            up, down = (z + step) % 16, (z - step) % 16
            table[z * 2, i] = (up % 4) * 4 + up // 4
            table[z * 2 + 1, i] = down
    return table


def gather(values, groups):
    copies = jnp.broadcast_to(values[None], (4,) + values.shape)
    parts = lax.all_to_all(copies, plane, 0, 0, axis_index_groups=groups)
    return parts.reshape((4 * values.shape[0],) + values.shape[1:])


def swap_cores(values):
    return lax.ppermute(values, "rep", [(0, 1), (1, 0), (2, 3), (3, 2)])


def send(values, distance):
    pairs = []
    for z in range(16):
        for rep in range(4):
            target = (z + (-distance if rep % 2 else distance)) % 16
            pairs.append((z * 4 + rep, target * 4 + rep))
    return lax.ppermute(values, ring, pairs)


def matmul_nt(a, b):
    return lax.dot_general(a, b, (((1,), (1,)), ((), ())), preferred_element_type=jnp.float32)


def matmul_tn(a, b):
    return lax.dot_general(a, b, (((0,), (0,)), ((), ())), preferred_element_type=jnp.float32)


def partial_kernel(groups, order_ref, grad_ref, own_ref, other_ref, out_ref):
    width = own_ref.shape[0]
    for start, count, flipped in groups:
        rows = jnp.concatenate([grad_ref[order_ref[start + i]] for i in range(count)], axis=0)
        for side, ref in enumerate((other_ref, own_ref) if flipped else (own_ref, other_ref)):
            part = matmul_nt(rows, ref[...]).astype(out_ref.dtype)
            out_ref[start : start + count, :, side * width : (side + 1) * width] = part.reshape(
                count, -1, width
            )


def partials(order, grad_blocks, weight_own, weight_other, groups):
    count = sum(g[1] for g in groups)
    rows, depth = grad_blocks.shape[1:]
    width = weight_own.shape[0]
    vmem = pl.BlockSpec(memory_space=pltpu.VMEM)
    return pl.pallas_call(
        functools.partial(partial_kernel, groups),
        out_shape=jax.ShapeDtypeStruct((count, rows, 2 * width), jnp.bfloat16),
        in_specs=[pl.BlockSpec(memory_space=pltpu.SMEM), vmem, vmem, vmem],
        out_specs=vmem,
        compiler_params=pltpu.CompilerParams(vmem_limit_bytes=32 * 1024 * 1024),
        cost_estimate=pl.CostEstimate(
            flops=4 * count * rows * depth * width,
            bytes_accessed=2 * (grad_blocks.size + 2 * width * depth + 2 * count * rows * width),
            transcendentals=0,
        ),
    )(order, grad_blocks, weight_own, weight_other)


def local(layer_input, weight, gelu_input, upstream):
    core = lax.axis_index("rep") % 2
    z = lax.axis_index("col")
    first = core == 0
    tokens, width = layer_input.shape
    half = tokens // 2
    f32, bf16 = jnp.float32, jnp.bfloat16

    input_whole = lax.all_gather(layer_input, "col", axis=0, tiled=True)
    weight_other = swap_cores(weight)
    gelu_grad = (upstream.astype(f32) * gelu_slope(gelu_input.astype(f32))).astype(bf16)

    line = gather(gelu_grad, along_x[0] + along_y[1])
    grad_tokens = gather(line, along_y[0] + along_x[1])
    grad_blocks = grad_tokens.reshape((16, half) + grad_tokens.shape[1:])

    early = lax.dynamic_index_in_dim(jnp.asarray(order_of(early_steps)), z * 2 + core, 0, False)
    late = lax.dynamic_index_in_dim(jnp.asarray(order_of(late_steps)), z * 2 + core, 0, False)
    ahead = partials(
        early, grad_blocks, weight, weight_other, ((0, 4, False), (4, 1, False), (5, 4, True))
    )
    from_sibling = swap_cores(ahead[5:])
    rest = partials(late, grad_blocks, weight, weight_other, ((0, 4, False), (4, 3, True)))
    rest_sibling = swap_cores(rest[4:])

    moved = send(jnp.concatenate([ahead[:4], from_sibling]), 1).reshape(2, 4, half, 2 * width)
    moved_far = send(ahead[4], 2)
    sums = [
        moved[:, i].astype(f32) + jnp.stack([rest[i], rest_sibling[i]]).astype(f32)
        for i in range(3)
    ]
    sums[0] = sums[0].at[0].add(moved_far.astype(f32))
    here = moved[:, 3].astype(f32).at[0].add(rest[3].astype(f32))
    moved = send(jnp.stack([sums[0], sums[2]]).astype(bf16), 2)
    moved, input_whole = lax.optimization_barrier((moved, input_whole))
    here = here + moved[1].astype(f32)
    moved = send((sums[1] + moved[0].astype(f32)).astype(bf16), 4)
    here = here + moved.astype(f32)

    from_other = swap_cores(here[:, :, width:].astype(bf16)).astype(f32)
    own = here[0, :, :width] + from_other[1]
    other = here[1, :, :width] + from_other[0]
    grad_input = jnp.where(
        first, jnp.concatenate([own, other]), jnp.concatenate([other, own])
    ).astype(bf16)

    blocks = input_whole.reshape(16, 2, half, width)
    mine = lax.dynamic_index_in_dim(blocks, core, 1, keepdims=False)
    other = swap_cores(lax.dynamic_index_in_dim(blocks, 1 - core, 1, keepdims=False))

    def ordered(values):
        chips = values.reshape(4, 4, half, width)
        return jnp.where(first, jnp.swapaxes(chips, 0, 1), chips).reshape(16 * half, width)

    sibling = swap_cores(matmul_tn(ordered(other), grad_tokens))
    grad_weight = matmul_tn(ordered(mine), grad_tokens) + sibling
    return (grad_input, grad_weight)


def solution(mesh):
    in_specs = (
        P("col", ("row", "rep")),
        P(("row", "rep"), "col"),
        P(("row", "rep"), "col"),
        P(("row", "rep"), "col"),
    )
    out_specs = (P("col", ("row", "rep")), P(("row", "rep"), "col"))
    return jax.shard_map(local, mesh=mesh, in_specs=in_specs, out_specs=out_specs, check_vma=False)
```

```python
import functools
import math

import jax
import jax.numpy as jnp
import numpy as np
from jax import lax
from jax.experimental import pallas as pl
from jax.experimental.pallas import tpu as pltpu
from jax.sharding import PartitionSpec as P

cubic_term = 0.044715
plane = ("row", "rep")
ring = ("col", "rep")


def gelu_slope(values):
    scale = math.sqrt(2.0 / math.pi)
    inner = scale * (values + cubic_term * values * values * values)
    tangent = jnp.tanh(inner)
    return 0.5 * (1.0 + tangent) + 0.5 * values * (1.0 - tangent * tangent) * scale * (
        1.0 + 3.0 * cubic_term * values * values
    )


def index(x, y, core):
    return ((x * 2 + y % 2) * 2 + y // 2) * 2 + core


y_order = (0, 2, 1, 3)
along_x = [[[index(x, y, core) for x in range(4)] for y in y_order] for core in range(2)]
along_y = [[[index(x, y, core) for y in y_order] for x in range(4)] for core in range(2)]


early_steps = (7, 5, 3, 1, 8, -7, -5, -3, -1)
late_steps = (6, 4, 2, 0, -6, -4, -2)
input_steps = (0, 2, 4, 6, 1, 3, 5, 7, 8, -2, -4, -6, -1, -3, -5, -7)


def order_of(steps):
    table = np.zeros((32, len(steps)), np.int32)
    for z in range(16):
        for i, step in enumerate(steps):
            up, down = (z + step) % 16, (z - step) % 16
            table[z * 2, i] = (up % 4) * 4 + up // 4
            table[z * 2 + 1, i] = down
    return table


def input_order():
    return np.argsort(order_of(input_steps), axis=1).astype(np.int32)


def gather(values, groups):
    copies = jnp.broadcast_to(values[None], (4,) + values.shape)
    parts = lax.all_to_all(copies, plane, 0, 0, axis_index_groups=groups)
    return parts.reshape((4 * values.shape[0],) + values.shape[1:])


def swap_cores(values):
    return lax.ppermute(values, "rep", [(0, 1), (1, 0), (2, 3), (3, 2)])


def send(values, distance):
    pairs = []
    for z in range(16):
        for rep in range(4):
            target = (z + (-distance if rep % 2 else distance)) % 16
            pairs.append((z * 4 + rep, target * 4 + rep))
    return lax.ppermute(values, ring, pairs)


def matmul_nt(a, b):
    return lax.dot_general(a, b, (((1,), (1,)), ((), ())), preferred_element_type=jnp.float32)


def matmul_tn(a, b):
    return lax.dot_general(a, b, (((0,), (0,)), ((), ())), preferred_element_type=jnp.float32)


def partial_kernel(groups, order_ref, grad_ref, own_ref, other_ref, out_ref):
    width = own_ref.shape[0]
    for start, count, flipped in groups:
        rows = jnp.concatenate([grad_ref[order_ref[start + i]] for i in range(count)], axis=0)
        for side, ref in enumerate((other_ref, own_ref) if flipped else (own_ref, other_ref)):
            part = matmul_nt(rows, ref[...]).astype(out_ref.dtype)
            out_ref[start : start + count, :, side * width : (side + 1) * width] = part.reshape(
                count, -1, width
            )


def partials(order, grad_blocks, weight_own, weight_other, groups):
    count = sum(g[1] for g in groups)
    rows, depth = grad_blocks.shape[1:]
    width = weight_own.shape[0]
    vmem = pl.BlockSpec(memory_space=pltpu.VMEM)
    return pl.pallas_call(
        functools.partial(partial_kernel, groups),
        out_shape=jax.ShapeDtypeStruct((count, rows, 2 * width), jnp.bfloat16),
        in_specs=[pl.BlockSpec(memory_space=pltpu.SMEM), vmem, vmem, vmem],
        out_specs=vmem,
        compiler_params=pltpu.CompilerParams(vmem_limit_bytes=32 * 1024 * 1024),
        cost_estimate=pl.CostEstimate(
            flops=4 * count * rows * depth * width,
            bytes_accessed=2 * (grad_blocks.size + 2 * width * depth + 2 * count * rows * width),
            transcendentals=0,
        ),
    )(order, grad_blocks, weight_own, weight_other)


def weight_kernel(side, add, order_ref, input_ref, grad_ref, *rest):
    sibling_ref = rest[0] if add else None
    out_ref, rows_ref = rest[-2:]
    width, half = out_ref.shape[0], input_ref.shape[1]
    for i in range(16):
        block = input_ref[order_ref[i]]
        rows_ref[i * half : (i + 1) * half, :] = block[:, side * width : (side + 1) * width]
    tile = 256
    for start in range(0, out_ref.shape[1], tile):
        grad = grad_ref[:, :, start : start + tile].reshape(16 * half, tile)
        part = matmul_tn(rows_ref[...], grad)
        if add:
            part = part + sibling_ref[:, start : start + tile]
        out_ref[:, start : start + tile] = part


def weight_part(order, input_blocks, grad_blocks, side, sibling=None):
    rows, both = input_blocks.shape[1:]
    width, depth = both // 2, grad_blocks.shape[2]
    vmem = pl.BlockSpec(memory_space=pltpu.VMEM)
    more = () if sibling is None else (sibling,)
    return pl.pallas_call(
        functools.partial(weight_kernel, side, sibling is not None),
        out_shape=jax.ShapeDtypeStruct((width, depth), jnp.float32),
        in_specs=[pl.BlockSpec(memory_space=pltpu.SMEM)] + [vmem] * (2 + len(more)),
        out_specs=vmem,
        scratch_shapes=[pltpu.VMEM((16 * rows, width), jnp.bfloat16)],
        compiler_params=pltpu.CompilerParams(vmem_limit_bytes=32 * 1024 * 1024),
        cost_estimate=pl.CostEstimate(
            flops=2 * 16 * rows * width * depth,
            bytes_accessed=2 * (grad_blocks.size + 16 * rows * width) + 4 * width * depth,
            transcendentals=0,
        ),
    )(order, input_blocks, grad_blocks, *more)


def local(layer_input, weight, gelu_input, upstream):
    core = lax.axis_index("rep") % 2
    z = lax.axis_index("col")
    first = core == 0
    tokens, width = layer_input.shape
    half = tokens // 2
    f32, bf16 = jnp.float32, jnp.bfloat16

    gelu_grad = (upstream.astype(f32) * gelu_slope(gelu_input.astype(f32))).astype(bf16)
    weight_other = swap_cores(weight)

    block = jnp.concatenate(
        [v.reshape(2, half, width) for v in (layer_input, swap_cores(layer_input))], axis=2
    )
    block = jnp.where(first, block, block[::-1])

    line = gather(gelu_grad, along_x[0] + along_y[1])
    input_4 = send(block, -4)
    line, input_4 = lax.optimization_barrier((line, input_4))
    grad_tokens = gather(line, along_y[0] + along_x[1])
    input_2_6 = send(jnp.stack([block, input_4]), -2)
    input_8 = send(input_4[0], -4)
    grad_tokens, input_2_6, input_8 = lax.optimization_barrier((grad_tokens, input_2_6, input_8))
    grad_blocks = grad_tokens.reshape((16, half) + grad_tokens.shape[1:])
    evens = jnp.stack([block, input_2_6[0], input_4, input_2_6[1]])
    odds = send(evens, -1)

    early = lax.dynamic_index_in_dim(jnp.asarray(order_of(early_steps)), z * 2 + core, 0, False)
    late = lax.dynamic_index_in_dim(jnp.asarray(order_of(late_steps)), z * 2 + core, 0, False)
    ahead = partials(
        early, grad_blocks, weight, weight_other, ((0, 4, False), (4, 1, False), (5, 4, True))
    )
    from_sibling = swap_cores(ahead[5:])
    rest = partials(late, grad_blocks, weight, weight_other, ((0, 4, False), (4, 3, True)))
    rest, odds = lax.optimization_barrier((rest, odds))
    rest_sibling = swap_cores(rest[4:])

    moved = send(jnp.concatenate([ahead[:4], from_sibling]), 1).reshape(2, 4, half, 2 * width)
    moved_far = send(ahead[4], 2)
    sums = [
        moved[:, i].astype(f32) + jnp.stack([rest[i], rest_sibling[i]]).astype(f32)
        for i in range(3)
    ]
    sums[0] = sums[0].at[0].add(moved_far.astype(f32))
    here = moved[:, 3].astype(f32).at[0].add(rest[3].astype(f32))
    moved = send(jnp.stack([sums[0], sums[2]]).astype(bf16), 2)
    here = here + moved[1].astype(f32)
    moved = send((sums[1] + moved[0].astype(f32)).astype(bf16), 4)

    others = jnp.concatenate([evens[1:, 1], odds[:, 1]])
    others = jnp.concatenate([others[:, :, width:], others[:, :, :width]], axis=2)
    input_blocks = jnp.concatenate([evens[:, 0], odds[:, 0], input_8[None], swap_cores(others)])
    order = lax.dynamic_index_in_dim(jnp.asarray(input_order()), z * 2 + core, 0, False)
    sibling = swap_cores(weight_part(order, input_blocks, grad_blocks, 1))
    grad_weight = weight_part(order, input_blocks, grad_blocks, 0, sibling)

    moved, grad_weight = lax.optimization_barrier((moved, grad_weight))
    here = here + moved.astype(f32)
    from_other = swap_cores(here[:, :, width:].astype(bf16)).astype(f32)
    own = here[0, :, :width] + from_other[1]
    other = here[1, :, :width] + from_other[0]
    grad_input = jnp.where(
        first, jnp.concatenate([own, other]), jnp.concatenate([other, own])
    ).astype(bf16)
    return (grad_input, grad_weight)


def solution(mesh):
    in_specs = (
        P("col", ("row", "rep")),
        P(("row", "rep"), "col"),
        P(("row", "rep"), "col"),
        P(("row", "rep"), "col"),
    )
    out_specs = (P("col", ("row", "rep")), P(("row", "rep"), "col"))
    return jax.shard_map(local, mesh=mesh, in_specs=in_specs, out_specs=out_specs, check_vma=False)
```

```python
import functools
import math

import jax
import jax.numpy as jnp
from jax import lax
from jax.experimental import pallas as pl
from jax.experimental.pallas import tpu as pltpu
from jax.sharding import PartitionSpec as P

cubic_term = 0.044715
plane = ("row", "rep")
ring = ("col", "rep")


def gelu_slope(values):
    scale = math.sqrt(2.0 / math.pi)
    inner = scale * (values + cubic_term * values * values * values)
    tangent = jnp.tanh(inner)
    return 0.5 * (1.0 + tangent) + 0.5 * values * (1.0 - tangent * tangent) * scale * (
        1.0 + 3.0 * cubic_term * values * values
    )


def index(x, y, core):
    return ((x * 2 + y % 2) * 2 + y // 2) * 2 + core


y_order = (0, 2, 1, 3)
along_x = [[[index(x, y, core) for x in range(4)] for y in y_order] for core in range(2)]
along_y = [[[index(x, y, core) for y in y_order] for x in range(4)] for core in range(2)]


early_steps = (7, 5, 3, 1, -7, -5, -3, -1, 8)
late_steps = (6, 4, 2, 0, -6, -4, -2)
input_steps = (0, 2, 4, 6, 1, 3, 5, 7, 8, -2, -4, -6, -1, -3, -5, -7)


def place(step):
    core = lax.rem(lax.axis_index("rep"), 2)
    chip = lax.rem(lax.axis_index("col") + (1 - 2 * core) * step + 16, 16)
    return jnp.where(core == 0, lax.rem(chip, 4) * 4 + lax.div(chip, 4), chip)


def gather(values, groups):
    copies = jnp.broadcast_to(values[None], (4,) + values.shape)
    parts = lax.all_to_all(copies, plane, 0, 0, axis_index_groups=groups)
    return parts.reshape((4 * values.shape[0],) + values.shape[1:])


def swap_cores(values):
    return lax.ppermute(values, "rep", [(0, 1), (1, 0), (2, 3), (3, 2)])


def send(values, distance, cross=False):
    pairs = []
    for z in range(16):
        for rep in range(4):
            target = (z + (-distance if rep % 2 else distance)) % 16
            pairs.append((z * 4 + rep, target * 4 + (rep ^ 1 if cross else rep)))
    return lax.ppermute(values, ring, pairs)


def matmul_nt(a, b):
    return lax.dot_general(a, b, (((1,), (1,)), ((), ())), preferred_element_type=jnp.float32)


def matmul_tn(a, b):
    return lax.dot_general(a, b, (((0,), (0,)), ((), ())), preferred_element_type=jnp.float32)


def partial_kernel(steps, groups, grad_ref, own_ref, other_ref, out_ref):
    width = own_ref.shape[0]
    for start, count, flipped in groups:
        rows = jnp.concatenate([grad_ref[place(steps[start + i])] for i in range(count)], axis=0)
        for side, ref in enumerate((other_ref, own_ref) if flipped else (own_ref, other_ref)):
            part = matmul_nt(rows, ref[...]).astype(out_ref.dtype)
            out_ref[start : start + count, :, side * width : (side + 1) * width] = part.reshape(
                count, -1, width
            )


def partials(steps, grad_blocks, weight_own, weight_other, groups):
    count = len(steps)
    rows, depth = grad_blocks.shape[1:]
    width = weight_own.shape[0]
    vmem = pl.BlockSpec(memory_space=pltpu.VMEM)
    return pl.pallas_call(
        functools.partial(partial_kernel, steps, groups),
        out_shape=jax.ShapeDtypeStruct((count, rows, 2 * width), jnp.bfloat16),
        in_specs=[vmem] * 3,
        out_specs=vmem,
        compiler_params=pltpu.CompilerParams(vmem_limit_bytes=32 * 1024 * 1024),
        cost_estimate=pl.CostEstimate(
            flops=4 * count * rows * depth * width,
            bytes_accessed=2 * (grad_blocks.size + 2 * width * depth + 2 * count * rows * width),
            transcendentals=0,
        ),
    )(grad_blocks, weight_own, weight_other)


def weight_kernel(side, add, evens_ref, odds_ref, far_ref, evens_other_ref, odds_other_ref,
                  grad_ref, *rest):
    sibling_ref = rest[0] if add else None
    out_ref, rows_ref = rest[-2:]
    width, half = out_ref.shape[0], far_ref.shape[0]
    sources = (
        [(evens_ref, (i, 0)) for i in range(4)]
        + [(odds_ref, (i,)) for i in range(4)]
        + [(far_ref, ())]
        + [(evens_other_ref, (i,)) for i in range(3)]
        + [(odds_other_ref, (i,)) for i in range(4)]
    )
    for (ref, at), step in zip(sources, input_steps):
        rows = pl.ds(pl.multiple_of(place(step) * half, half), half)
        rows_ref[rows, :] = ref[at + (slice(None), slice(side * width, (side + 1) * width))]
    tile = 256
    for start in range(0, out_ref.shape[1], tile):
        grad = grad_ref[:, :, start : start + tile].reshape(16 * half, tile)
        part = matmul_tn(rows_ref[...], grad)
        if add:
            part = part + sibling_ref[:, start : start + tile].astype(jnp.float32)
        out_ref[:, start : start + tile] = part.astype(out_ref.dtype)


def weight_part(input_blocks, grad_blocks, side, dtype, sibling=None):
    rows, both = input_blocks[2].shape
    width, depth = both // 2, grad_blocks.shape[2]
    vmem = pl.BlockSpec(memory_space=pltpu.VMEM)
    more = () if sibling is None else (sibling,)
    return pl.pallas_call(
        functools.partial(weight_kernel, side, sibling is not None),
        out_shape=jax.ShapeDtypeStruct((width, depth), dtype),
        in_specs=[vmem] * (6 + len(more)),
        out_specs=vmem,
        scratch_shapes=[pltpu.VMEM((16 * rows, width), jnp.bfloat16)],
        compiler_params=pltpu.CompilerParams(vmem_limit_bytes=32 * 1024 * 1024),
        cost_estimate=pl.CostEstimate(
            flops=2 * 16 * rows * width * depth,
            bytes_accessed=2 * (grad_blocks.size + 16 * rows * width) + 4 * width * depth,
            transcendentals=0,
        ),
    )(*input_blocks, grad_blocks, *more)


def local(layer_input, weight, gelu_input, upstream):
    core = lax.axis_index("rep") % 2
    first = core == 0
    tokens, width = layer_input.shape
    half = tokens // 2
    f32, bf16 = jnp.float32, jnp.bfloat16

    gelu_grad = (upstream.astype(f32) * gelu_slope(gelu_input.astype(f32))).astype(bf16)
    weight_other = swap_cores(weight)

    block = jnp.concatenate(
        [v.reshape(2, half, width) for v in (layer_input, swap_cores(layer_input))], axis=2
    )
    block = jnp.where(first, block, block[::-1])

    gelu_grad, block = lax.optimization_barrier((gelu_grad, block))
    line = gather(gelu_grad, along_x[0] + along_y[1])
    input_4 = send(block, -4)
    line, input_4 = lax.optimization_barrier((line, input_4))
    grad_tokens = gather(line, along_y[0] + along_x[1])
    input_2_6 = send(jnp.stack([block, input_4]), -2)
    input_8 = send(input_4[0], -4)
    grad_tokens, input_2_6 = lax.optimization_barrier((grad_tokens, input_2_6))
    evens = jnp.stack([block, input_2_6[0], input_4, input_2_6[1]])
    flipped = jnp.concatenate([evens[:, 1, :, width:], evens[:, 1, :, :width]], axis=2)
    odds = send(evens[:, 0], -1)
    odds_other = send(flipped, -1, cross=True)
    evens_other = swap_cores(flipped[1:])
    grad_blocks = grad_tokens.reshape((16, half) + grad_tokens.shape[1:])

    ahead = partials(
        early_steps, grad_blocks, weight, weight_other, ((0, 4, False), (4, 4, True), (8, 1, False))
    )
    ahead, later_blocks = lax.optimization_barrier((ahead, grad_blocks))
    moved = (send(ahead[:4], 1), send(ahead[4:8], -1, cross=True))
    moved_far = send(ahead[8], 4)
    rest = partials(late_steps, later_blocks, weight, weight_other, ((0, 4, False), (4, 3, True)))
    rest_sibling = swap_cores(rest[4:])
    input_blocks = (evens, odds, input_8, evens_other, odds_other)
    moved, rest, rest_sibling, input_blocks = lax.optimization_barrier(
        (moved, rest, rest_sibling, input_blocks)
    )

    sums = [
        jnp.stack([m[i].astype(f32) + r[i].astype(f32) for m, r in zip(moved, (rest, rest_sibling))])
        for i in range(3)
    ]
    here = jnp.stack([moved[0][3].astype(f32) + rest[3].astype(f32), moved[1][3].astype(f32)])
    moved = send(jnp.stack([sums[0], sums[2]]).astype(bf16), 2)
    for_sibling = weight_part(input_blocks, grad_blocks, 1, bf16)
    moved, moved_far, for_sibling = lax.optimization_barrier((moved, moved_far, for_sibling))
    here = here + moved[1].astype(f32)
    last = (sums[1] + moved[0].astype(f32)).at[0].add(moved_far.astype(f32)).astype(bf16)
    moved = send(last[:, :, :width], 4)
    moved_cross = send(last[:, :, width:], 4, cross=True)
    here_cross = swap_cores(here[:, :, width:].astype(bf16))

    sibling = swap_cores(for_sibling)
    grad_weight = weight_part(input_blocks, grad_blocks, 0, f32, sibling)

    moved, grad_weight = lax.optimization_barrier((moved, grad_weight))
    cross = moved_cross.astype(f32) + here_cross.astype(f32)
    summed = here[:, :, :width] + moved.astype(f32) + cross[::-1]
    own, other = summed[0], summed[1]
    grad_input = jnp.where(
        first, jnp.concatenate([own, other]), jnp.concatenate([other, own])
    ).astype(bf16)
    return (grad_input, grad_weight)


def solution(mesh):
    in_specs = (
        P("col", ("row", "rep")),
        P(("row", "rep"), "col"),
        P(("row", "rep"), "col"),
        P(("row", "rep"), "col"),
    )
    out_specs = (P("col", ("row", "rep")), P(("row", "rep"), "col"))
    return jax.shard_map(local, mesh=mesh, in_specs=in_specs, out_specs=out_specs, check_vma=False)
```

```python
import functools
import math

import jax
import jax.numpy as jnp
from jax import lax
from jax.experimental import pallas as pl
from jax.experimental.pallas import tpu as pltpu
from jax.sharding import PartitionSpec as P

cubic_term = 0.044715
plane = ("row", "rep")
ring = ("col", "rep")


def gelu_slope(values):
    scale = math.sqrt(2.0 / math.pi)
    inner = scale * (values + cubic_term * values * values * values)
    tangent = jnp.tanh(inner)
    return 0.5 * (1.0 + tangent) + 0.5 * values * (1.0 - tangent * tangent) * scale * (
        1.0 + 3.0 * cubic_term * values * values
    )


def index(x, y, core):
    return ((x * 2 + y % 2) * 2 + y // 2) * 2 + core


y_order = (0, 2, 1, 3)
along_x = [[[index(x, y, core) for x in range(4)] for y in y_order] for core in range(2)]
along_y = [[[index(x, y, core) for y in y_order] for x in range(4)] for core in range(2)]


early_steps = (7, 5, 3, 1, -7, -5, -3, -1, 8)
late_steps = (6, 4, 2, 0, -6, -4, -2)


def place(step):
    core = lax.rem(lax.axis_index("rep"), 2)
    chip = lax.rem(lax.axis_index("col") + (1 - 2 * core) * step + 16, 16)
    return jnp.where(core == 0, lax.rem(chip, 4) * 4 + lax.div(chip, 4), chip)


def gather(values, groups):
    copies = jnp.broadcast_to(values[None], (4,) + values.shape)
    parts = lax.all_to_all(copies, plane, 0, 0, axis_index_groups=groups)
    return parts.reshape((4 * values.shape[0],) + values.shape[1:])


def swap_cores(values):
    return lax.ppermute(values, "rep", [(0, 1), (1, 0), (2, 3), (3, 2)])


def gather_plane(gelu_grad, weight):
    line = gather(gelu_grad, along_x[0] + along_y[1])
    grad_tokens = gather(line, along_y[0] + along_x[1])
    return grad_tokens, swap_cores(weight)


def send(values, distance, cross=False):
    pairs = []
    for z in range(16):
        for rep in range(4):
            target = (z + (-distance if rep % 2 else distance)) % 16
            pairs.append((z * 4 + rep, target * 4 + (rep ^ 1 if cross else rep)))
    return lax.ppermute(values, ring, pairs)


def matmul_nt(a, b):
    return lax.dot_general(a, b, (((1,), (1,)), ((), ())), preferred_element_type=jnp.float32)


def matmul_tn(a, b):
    return lax.dot_general(a, b, (((0,), (0,)), ((), ())), preferred_element_type=jnp.float32)


def partial_kernel(steps, groups, grad_ref, own_ref, other_ref, out_ref):
    width = own_ref.shape[0]
    for start, count, flipped in groups:
        rows = jnp.concatenate([grad_ref[place(steps[start + i])] for i in range(count)], axis=0)
        for side, ref in enumerate((other_ref, own_ref) if flipped else (own_ref, other_ref)):
            part = matmul_nt(rows, ref[...]).astype(out_ref.dtype)
            out_ref[start : start + count, :, side * width : (side + 1) * width] = part.reshape(
                count, -1, width
            )


def partials(steps, grad_blocks, weight_own, weight_other, groups):
    count = len(steps)
    rows, depth = grad_blocks.shape[1:]
    width = weight_own.shape[0]
    vmem = pl.BlockSpec(memory_space=pltpu.VMEM)
    return pl.pallas_call(
        functools.partial(partial_kernel, steps, groups),
        out_shape=jax.ShapeDtypeStruct((count, rows, 2 * width), jnp.bfloat16),
        in_specs=[vmem] * 3,
        out_specs=vmem,
        compiler_params=pltpu.CompilerParams(vmem_limit_bytes=32 * 1024 * 1024),
        cost_estimate=pl.CostEstimate(
            flops=4 * count * rows * depth * width,
            bytes_accessed=2 * (grad_blocks.size + 2 * width * depth + 2 * count * rows * width),
            transcendentals=0,
        ),
    )(grad_blocks, weight_own, weight_other)


def weight_kernel(input_ref, grad_ref, other_ref, out_ref, rows_ref):
    half, depth = grad_ref.shape[1:]
    core = lax.rem(lax.axis_index("rep"), 2)
    for chip in range(16):
        turned = (chip % 4) * 4 + chip // 4
        own_at = jnp.where(core == 0, turned, chip)
        other_at = jnp.where(core == 0, chip, turned) + 16
        for at, tokens in ((own_at, core), (other_at, 1 - core)):
            rows = pl.ds(pl.multiple_of(at * half, half), half)
            rows_ref[rows, :] = input_ref[chip, tokens]
    tile = 256
    for start in range(0, depth, tile):
        out_ref[:, start : start + tile] = sum(
            matmul_tn(
                rows_ref[16 * half * i : 16 * half * (i + 1), :],
                ref[:, :, start : start + tile].reshape(16 * half, tile),
            )
            for i, ref in enumerate((grad_ref, other_ref))
        )


def weight_gradient(input_whole, grad_blocks, grad_other):
    tokens, width = input_whole.shape
    half, depth = grad_blocks.shape[1:]
    vmem = pl.BlockSpec(memory_space=pltpu.VMEM)
    return pl.pallas_call(
        weight_kernel,
        out_shape=jax.ShapeDtypeStruct((width, depth), jnp.float32),
        in_specs=[vmem] * 3,
        out_specs=vmem,
        scratch_shapes=[pltpu.VMEM((tokens, width), jnp.bfloat16)],
        compiler_params=pltpu.CompilerParams(vmem_limit_bytes=40 * 1024 * 1024),
        cost_estimate=pl.CostEstimate(
            flops=2 * tokens * width * depth,
            bytes_accessed=2 * tokens * (width + depth) + 4 * width * depth,
            transcendentals=0,
        ),
    )(input_whole.reshape(16, 2, half, width), grad_blocks, grad_other)


def local(layer_input, weight, gelu_input, upstream):
    first = lax.axis_index("rep") % 2 == 0
    tokens, width = layer_input.shape
    half = tokens // 2
    f32, bf16 = jnp.float32, jnp.bfloat16

    input_whole = lax.all_gather(layer_input, "col", axis=0, tiled=True)
    gelu_grad = (upstream.astype(f32) * gelu_slope(gelu_input.astype(f32))).astype(bf16)

    grad_tokens, weight_other = lax.cond(
        lax.axis_index("col") < 16,
        gather_plane,
        lambda g, w: (jnp.zeros((16 * half, g.shape[1]), g.dtype), jnp.zeros_like(w)),
        gelu_grad,
        weight,
    )
    grad_blocks = grad_tokens.reshape((16, half) + grad_tokens.shape[1:])
    grad_other = swap_cores(grad_blocks)

    ahead = partials(
        early_steps, grad_blocks, weight, weight_other, ((0, 4, False), (4, 4, True), (8, 1, False))
    )
    ahead, later_blocks = lax.optimization_barrier((ahead, grad_blocks))
    moved = (send(ahead[:4], 1), send(ahead[4:8], -1, cross=True))
    moved_far = send(ahead[8], 2)
    rest = partials(late_steps, later_blocks, weight, weight_other, ((0, 4, False), (4, 3, True)))
    rest_sibling = swap_cores(rest[4:])
    moved, moved_far, rest, rest_sibling = lax.optimization_barrier(
        (moved, moved_far, rest, rest_sibling)
    )

    sums = [
        jnp.stack([m[i].astype(f32) + r[i].astype(f32) for m, r in zip(moved, (rest, rest_sibling))])
        for i in range(3)
    ]
    sums[0] = sums[0].at[0].add(moved_far.astype(f32))
    here = jnp.stack([moved[0][3].astype(f32) + rest[3].astype(f32), moved[1][3].astype(f32)])
    moved = send(jnp.stack([sums[0], sums[2]]).astype(bf16), 2)
    moved, input_whole = lax.optimization_barrier((moved, input_whole))
    here = here + moved[1].astype(f32)
    last = (sums[1] + moved[0].astype(f32)).astype(bf16)
    moved = send(last[:, :, :width], 4)
    moved_cross = send(last[:, :, width:], 4, cross=True)
    here_cross = swap_cores(here[:, :, width:].astype(bf16))

    grad_weight = weight_gradient(input_whole, grad_blocks, grad_other)
    moved, grad_weight = lax.optimization_barrier((moved, grad_weight))
    cross = moved_cross.astype(f32) + here_cross.astype(f32)
    summed = here[:, :, :width] + moved.astype(f32) + cross[::-1]
    own, other = summed[0], summed[1]
    grad_input = jnp.where(
        first, jnp.concatenate([own, other]), jnp.concatenate([other, own])
    ).astype(bf16)
    return (grad_input, grad_weight)


def solution(mesh):
    in_specs = (
        P("col", ("row", "rep")),
        P(("row", "rep"), "col"),
        P(("row", "rep"), "col"),
        P(("row", "rep"), "col"),
    )
    out_specs = (P("col", ("row", "rep")), P(("row", "rep"), "col"))
    return jax.shard_map(local, mesh=mesh, in_specs=in_specs, out_specs=out_specs, check_vma=False)
```

```python
import functools
import math

import jax
import jax.numpy as jnp
from jax import lax
from jax.experimental import pallas as pl
from jax.experimental.pallas import tpu as pltpu
from jax.sharding import PartitionSpec as P

cubic_term = 0.044715
plane = ("row", "rep")
ring = ("col", "rep")


def gelu_slope(values):
    scale = math.sqrt(2.0 / math.pi)
    inner = scale * (values + cubic_term * values * values * values)
    tangent = jnp.tanh(inner)
    return 0.5 * (1.0 + tangent) + 0.5 * values * (1.0 - tangent * tangent) * scale * (
        1.0 + 3.0 * cubic_term * values * values
    )


def index(x, y, core):
    return ((x * 2 + y % 2) * 2 + y // 2) * 2 + core


y_order = (0, 2, 1, 3)
along_x = [[[index(x, y, core) for x in range(4)] for y in y_order] for core in range(2)]
along_y = [[[index(x, y, core) for y in y_order] for x in range(4)] for core in range(2)]


early_groups = (((7, 5, 3, 1), False), ((-7, -5, -3, -1), True), ((8,), False))
late_groups = (((6, 4, 2, 0), False), ((-6, -4, -2), True))


def place(step):
    core = lax.rem(lax.axis_index("rep"), 2)
    chip = lax.rem(lax.axis_index("col") + (1 - 2 * core) * step + 16, 16)
    return jnp.where(core == 0, lax.rem(chip, 4) * 4 + lax.div(chip, 4), chip)


def gather(values, groups):
    copies = jnp.broadcast_to(values[None], (4,) + values.shape)
    parts = lax.all_to_all(copies, plane, 0, 0, axis_index_groups=groups)
    return parts.reshape((4 * values.shape[0],) + values.shape[1:])


def swap_cores(values):
    return lax.ppermute(values, "rep", [(0, 1), (1, 0), (2, 3), (3, 2)])


def first_round(gelu_grad, weight):
    line = gather(gelu_grad, along_x[0] + along_y[1])
    grad_tokens = gather(line, along_y[0] + along_x[1])
    weight_other = swap_cores(weight)
    grad_blocks = grad_tokens.reshape((16, gelu_grad.shape[0], gelu_grad.shape[1]))

    ahead = partials(early_groups, grad_blocks, weight, weight_other)
    ahead, later_blocks = lax.optimization_barrier((ahead, grad_blocks))
    moved = send(ahead[0], 1), send(ahead[1], -1, cross=True), send(ahead[2], 2)
    rest, for_sibling = partials(late_groups, later_blocks, weight, weight_other)
    rest_sibling = swap_cores(for_sibling)
    rest, later_blocks = lax.optimization_barrier((rest, later_blocks))
    grad_other = swap_cores(later_blocks)

    both = (2,) + rest.shape[1:]
    outs = [
        jax.ShapeDtypeStruct((2,) + both, jnp.bfloat16),
        jax.ShapeDtypeStruct(both, jnp.float32),
        jax.ShapeDtypeStruct(both, jnp.float32),
    ]
    sums = call(first_kernel, outs, (*moved, rest, rest_sibling))
    return (*sums, grad_blocks, grad_other)


def send(values, distance, cross=False):
    pairs = []
    for z in range(16):
        for rep in range(4):
            target = (z + (-distance if rep % 2 else distance)) % 16
            pairs.append((z * 4 + rep, target * 4 + (rep ^ 1 if cross else rep)))
    return lax.ppermute(values, ring, pairs)


def matmul_nt(a, b):
    return lax.dot_general(a, b, (((1,), (1,)), ((), ())), preferred_element_type=jnp.float32)


def matmul_tn(a, b):
    return lax.dot_general(a, b, (((0,), (0,)), ((), ())), preferred_element_type=jnp.float32)


def call(kernel, outs, args, flops=0):
    vmem = pl.BlockSpec(memory_space=pltpu.VMEM)
    moved = sum(v.size * v.dtype.itemsize for v in tuple(args) + tuple(outs))
    return pl.pallas_call(
        kernel,
        out_shape=outs,
        in_specs=[vmem] * len(args),
        out_specs=tuple(vmem for _ in outs),
        compiler_params=pltpu.CompilerParams(vmem_limit_bytes=32 * 1024 * 1024),
        cost_estimate=pl.CostEstimate(flops=flops, bytes_accessed=moved, transcendentals=0),
    )(*args)


def partial_kernel(groups, grad_ref, own_ref, other_ref, *outs):
    width = own_ref.shape[0]
    for (steps, flipped), out_ref in zip(groups, outs):
        rows = jnp.concatenate([grad_ref[place(step)] for step in steps], axis=0)
        for side, ref in enumerate((other_ref, own_ref) if flipped else (own_ref, other_ref)):
            part = matmul_nt(rows, ref[...]).astype(out_ref.dtype)
            out_ref[:, :, side * width : (side + 1) * width] = part.reshape(len(steps), -1, width)


def partials(groups, grad_blocks, weight_own, weight_other):
    rows, depth = grad_blocks.shape[1:]
    width = weight_own.shape[0]
    outs = [jax.ShapeDtypeStruct((len(g[0]), rows, 2 * width), jnp.bfloat16) for g in groups]
    return call(
        functools.partial(partial_kernel, groups),
        outs,
        (grad_blocks, weight_own, weight_other),
        flops=4 * sum(len(g[0]) for g in groups) * rows * depth * width,
    )


def first_kernel(own_ref, cross_ref, far_ref, rest_ref, other_ref, send_ref, middle_ref, here_ref):
    def total(i, *refs):
        return sum(ref[i].astype(jnp.float32) for ref in refs)

    dtype = send_ref.dtype
    send_ref[0, 0] = (total(0, own_ref, rest_ref) + far_ref[0].astype(jnp.float32)).astype(dtype)
    send_ref[0, 1] = total(0, cross_ref, other_ref).astype(dtype)
    send_ref[1, 0] = total(2, own_ref, rest_ref).astype(dtype)
    send_ref[1, 1] = total(2, cross_ref, other_ref).astype(dtype)
    middle_ref[0] = total(1, own_ref, rest_ref)
    middle_ref[1] = total(1, cross_ref, other_ref)
    here_ref[0] = total(3, own_ref, rest_ref)
    here_ref[1] = total(3, cross_ref)


def second_kernel(moved_ref, middle_ref, here_ref, own_ref, cross_ref, stay_ref, swap_ref):
    width = own_ref.shape[2]
    ahead = (middle_ref[...] + moved_ref[0].astype(jnp.float32)).astype(own_ref.dtype)
    own_ref[...] = ahead[:, :, :width]
    cross_ref[...] = ahead[:, :, width:]
    here = here_ref[...] + moved_ref[1].astype(jnp.float32)
    stay_ref[...] = here[:, :, :width]
    swap_ref[...] = here[:, :, width:].astype(swap_ref.dtype)


def third_kernel(own_ref, cross_ref, stay_ref, swap_ref, out_ref):
    half = own_ref.shape[1]
    core = lax.rem(lax.axis_index("rep"), 2)
    for i, place_of in enumerate((core, 1 - core)):
        other = cross_ref[1 - i].astype(jnp.float32) + swap_ref[1 - i].astype(jnp.float32)
        part = stay_ref[i] + own_ref[i].astype(jnp.float32) + other
        rows = pl.ds(pl.multiple_of(place_of * half, half), half)
        out_ref[rows, :] = part.astype(out_ref.dtype)


def weight_kernel(input_ref, grad_ref, other_ref, out_ref, rows_ref):
    half, depth = grad_ref.shape[1:]
    core = lax.rem(lax.axis_index("rep"), 2)
    for chip in range(16):
        turned = (chip % 4) * 4 + chip // 4
        own_at = jnp.where(core == 0, turned, chip)
        other_at = jnp.where(core == 0, chip, turned) + 16
        for at, tokens in ((own_at, core), (other_at, 1 - core)):
            rows = pl.ds(pl.multiple_of(at * half, half), half)
            rows_ref[rows, :] = input_ref[chip, tokens]
    tile = 256
    for start in range(0, depth, tile):
        out_ref[:, start : start + tile] = sum(
            matmul_tn(
                rows_ref[16 * half * i : 16 * half * (i + 1), :],
                ref[:, :, start : start + tile].reshape(16 * half, tile),
            )
            for i, ref in enumerate((grad_ref, other_ref))
        )


def weight_gradient(input_whole, grad_blocks, grad_other):
    tokens, width = input_whole.shape
    half, depth = grad_blocks.shape[1:]
    vmem = pl.BlockSpec(memory_space=pltpu.VMEM)
    return pl.pallas_call(
        weight_kernel,
        out_shape=jax.ShapeDtypeStruct((width, depth), jnp.float32),
        in_specs=[vmem] * 3,
        out_specs=vmem,
        scratch_shapes=[pltpu.VMEM((tokens, width), jnp.bfloat16)],
        compiler_params=pltpu.CompilerParams(vmem_limit_bytes=40 * 1024 * 1024),
        cost_estimate=pl.CostEstimate(
            flops=2 * tokens * width * depth,
            bytes_accessed=2 * tokens * (width + depth) + 4 * width * depth,
            transcendentals=0,
        ),
    )(input_whole.reshape(16, 2, half, width), grad_blocks, grad_other)


def local(layer_input, weight, gelu_input, upstream):
    tokens, width = layer_input.shape
    half = tokens // 2
    f32, bf16 = jnp.float32, jnp.bfloat16

    input_whole = lax.all_gather(layer_input, "col", axis=0, tiled=True)
    gelu_grad = (upstream.astype(f32) * gelu_slope(gelu_input.astype(f32))).astype(bf16)

    both, blocks = (2, half, 2 * width), (16, half, gelu_grad.shape[1])
    shapes = (((2,) + both, bf16), (both, f32), (both, f32), (blocks, bf16), (blocks, bf16))
    to_send, middle, here, grad_blocks, grad_other = lax.cond(
        lax.axis_index("col") < 16,
        first_round,
        lambda g, w: tuple(jnp.zeros(*v) for v in shapes),
        gelu_grad,
        weight,
    )

    moved = send(to_send, 2)
    grad_weight = weight_gradient(input_whole, grad_blocks, grad_other)
    moved, grad_weight = lax.optimization_barrier((moved, grad_weight))
    part = (2, half, width)
    outs = [jax.ShapeDtypeStruct(part, t) for t in (bf16, bf16, f32, bf16)]
    own, cross, stay, swapped = call(second_kernel, outs, (moved, middle, here))
    last = send(own, 4), send(cross, 4, cross=True), stay, swap_cores(swapped)
    outs = [jax.ShapeDtypeStruct((tokens, width), bf16)]
    grad_input = call(third_kernel, outs, last)[0]
    return (grad_input, grad_weight)


def solution(mesh):
    in_specs = (
        P("col", ("row", "rep")),
        P(("row", "rep"), "col"),
        P(("row", "rep"), "col"),
        P(("row", "rep"), "col"),
    )
    out_specs = (P("col", ("row", "rep")), P(("row", "rep"), "col"))
    return jax.shard_map(local, mesh=mesh, in_specs=in_specs, out_specs=out_specs, check_vma=False)
```

```python
import functools
import math

import jax
import jax.numpy as jnp
from jax import lax
from jax.experimental import pallas as pl
from jax.experimental.pallas import tpu as pltpu
from jax.sharding import PartitionSpec as P

cubic_term = 0.044715
plane = ("row", "rep")
ring = ("col", "rep")


def gelu_slope(values):
    scale = math.sqrt(2.0 / math.pi)
    inner = scale * (values + cubic_term * values * values * values)
    tangent = jnp.tanh(inner)
    return 0.5 * (1.0 + tangent) + 0.5 * values * (1.0 - tangent * tangent) * scale * (
        1.0 + 3.0 * cubic_term * values * values
    )


def index(x, y, core):
    return ((x * 2 + y % 2) * 2 + y // 2) * 2 + core


y_order = (0, 2, 1, 3)
along_x = [[[index(x, y, core) for x in range(4)] for y in y_order] for core in range(2)]
along_y = [[[index(x, y, core) for y in y_order] for x in range(4)] for core in range(2)]


early_groups = (((7, 5, 3, 1), False), ((-7, -5, -3, -1), True), ((8,), False))
late_groups = (((6, 4, 2, 0), False), ((-6, -4, -2), True))


def place(step):
    core = lax.rem(lax.axis_index("rep"), 2)
    chip = lax.rem(lax.axis_index("col") + (1 - 2 * core) * step + 16, 16)
    return jnp.where(core == 0, lax.rem(chip, 4) * 4 + lax.div(chip, 4), chip)


def gather(values, groups):
    copies = jnp.broadcast_to(values[None], (4,) + values.shape)
    parts = lax.all_to_all(copies, plane, 0, 0, axis_index_groups=groups)
    return parts.reshape((4 * values.shape[0],) + values.shape[1:])


def swap_cores(values):
    return lax.ppermute(values, "rep", [(0, 1), (1, 0), (2, 3), (3, 2)])


def first_round(gelu_grad, weight):
    line = gather(gelu_grad, along_x[0] + along_y[1])
    grad_tokens = gather(line, along_y[0] + along_x[1])
    weight_other = swap_cores(weight)
    grad_blocks = grad_tokens.reshape((16, gelu_grad.shape[0], gelu_grad.shape[1]))

    ahead = partials(early_groups, grad_blocks, weight, weight_other)
    ahead, later_blocks = lax.optimization_barrier((ahead, grad_blocks))
    moved = send(ahead[0], 1), send(ahead[1], -1, cross=True), send(ahead[2], 2)
    rest, for_sibling = partials(late_groups, later_blocks, weight, weight_other)
    rest_sibling = swap_cores(for_sibling)
    grad_other = swap_cores(later_blocks)

    both = (2,) + rest.shape[1:]
    outs = [
        jax.ShapeDtypeStruct((2,) + both, jnp.bfloat16),
        jax.ShapeDtypeStruct(both, jnp.float32),
        jax.ShapeDtypeStruct(both, jnp.float32),
    ]
    sums = call(first_kernel, outs, (*moved, rest, rest_sibling))
    return (*sums, grad_blocks, grad_other)


def send(values, distance, cross=False):
    pairs = []
    for z in range(16):
        for rep in range(4):
            target = (z + (-distance if rep % 2 else distance)) % 16
            pairs.append((z * 4 + rep, target * 4 + (rep ^ 1 if cross else rep)))
    return lax.ppermute(values, ring, pairs)


def matmul_nt(a, b):
    return lax.dot_general(a, b, (((1,), (1,)), ((), ())), preferred_element_type=jnp.float32)


def matmul_tn(a, b):
    return lax.dot_general(a, b, (((0,), (0,)), ((), ())), preferred_element_type=jnp.float32)


def call(kernel, outs, args, flops=0):
    vmem = pl.BlockSpec(memory_space=pltpu.VMEM)
    moved = sum(v.size * v.dtype.itemsize for v in tuple(args) + tuple(outs))
    return pl.pallas_call(
        kernel,
        out_shape=outs,
        in_specs=[vmem] * len(args),
        out_specs=tuple(vmem for _ in outs),
        compiler_params=pltpu.CompilerParams(vmem_limit_bytes=32 * 1024 * 1024),
        cost_estimate=pl.CostEstimate(flops=flops, bytes_accessed=moved, transcendentals=0),
    )(*args)


def partial_kernel(groups, grad_ref, own_ref, other_ref, *outs):
    width = own_ref.shape[0]
    for (steps, flipped), out_ref in zip(groups, outs):
        rows = jnp.concatenate([grad_ref[place(step)] for step in steps], axis=0)
        for side, ref in enumerate((other_ref, own_ref) if flipped else (own_ref, other_ref)):
            part = matmul_nt(rows, ref[...]).astype(out_ref.dtype)
            out_ref[:, :, side * width : (side + 1) * width] = part.reshape(len(steps), -1, width)


def partials(groups, grad_blocks, weight_own, weight_other):
    rows, depth = grad_blocks.shape[1:]
    width = weight_own.shape[0]
    outs = [jax.ShapeDtypeStruct((len(g[0]), rows, 2 * width), jnp.bfloat16) for g in groups]
    return call(
        functools.partial(partial_kernel, groups),
        outs,
        (grad_blocks, weight_own, weight_other),
        flops=4 * sum(len(g[0]) for g in groups) * rows * depth * width,
    )


def first_kernel(own_ref, cross_ref, far_ref, rest_ref, other_ref, send_ref, middle_ref, here_ref):
    def total(i, *refs):
        return sum(ref[i].astype(jnp.float32) for ref in refs)

    dtype = send_ref.dtype
    send_ref[0, 0] = (total(0, own_ref, rest_ref) + far_ref[0].astype(jnp.float32)).astype(dtype)
    send_ref[0, 1] = total(0, cross_ref, other_ref).astype(dtype)
    send_ref[1, 0] = total(2, own_ref, rest_ref).astype(dtype)
    send_ref[1, 1] = total(2, cross_ref, other_ref).astype(dtype)
    middle_ref[0] = total(1, own_ref, rest_ref)
    middle_ref[1] = total(1, cross_ref, other_ref)
    here_ref[0] = total(3, own_ref, rest_ref)
    here_ref[1] = total(3, cross_ref)


def second_kernel(moved_ref, middle_ref, here_ref, own_ref, cross_ref, stay_ref, swap_ref):
    width = own_ref.shape[2]
    ahead = (middle_ref[...] + moved_ref[0].astype(jnp.float32)).astype(own_ref.dtype)
    own_ref[...] = ahead[:, :, :width]
    cross_ref[...] = ahead[:, :, width:]
    here = here_ref[...] + moved_ref[1].astype(jnp.float32)
    stay_ref[...] = here[:, :, :width]
    swap_ref[...] = here[:, :, width:].astype(swap_ref.dtype)


def third_kernel(own_ref, cross_ref, stay_ref, swap_ref, out_ref):
    half = own_ref.shape[1]
    core = lax.rem(lax.axis_index("rep"), 2)
    for i, place_of in enumerate((core, 1 - core)):
        other = cross_ref[1 - i].astype(jnp.float32) + swap_ref[1 - i].astype(jnp.float32)
        part = stay_ref[i] + own_ref[i].astype(jnp.float32) + other
        rows = pl.ds(pl.multiple_of(place_of * half, half), half)
        out_ref[rows, :] = part.astype(out_ref.dtype)


def weight_kernel(input_ref, grad_ref, other_ref, out_ref, rows_ref):
    half, depth = grad_ref.shape[1:]
    core = lax.rem(lax.axis_index("rep"), 2)
    for chip in range(16):
        turned = (chip % 4) * 4 + chip // 4
        own_at = jnp.where(core == 0, turned, chip)
        other_at = jnp.where(core == 0, chip, turned) + 16
        for at, tokens in ((own_at, core), (other_at, 1 - core)):
            rows = pl.ds(pl.multiple_of(at * half, half), half)
            rows_ref[rows, :] = input_ref[chip, tokens]
    tile = 256
    for start in range(0, depth, tile):
        out_ref[:, start : start + tile] = sum(
            matmul_tn(
                rows_ref[16 * half * i : 16 * half * (i + 1), :],
                ref[:, :, start : start + tile].reshape(16 * half, tile),
            )
            for i, ref in enumerate((grad_ref, other_ref))
        )


def weight_gradient(input_whole, grad_blocks, grad_other):
    tokens, width = input_whole.shape
    half, depth = grad_blocks.shape[1:]
    vmem = pl.BlockSpec(memory_space=pltpu.VMEM)
    return pl.pallas_call(
        weight_kernel,
        out_shape=jax.ShapeDtypeStruct((width, depth), jnp.float32),
        in_specs=[vmem] * 3,
        out_specs=vmem,
        scratch_shapes=[pltpu.VMEM((tokens, width), jnp.bfloat16)],
        compiler_params=pltpu.CompilerParams(vmem_limit_bytes=40 * 1024 * 1024),
        cost_estimate=pl.CostEstimate(
            flops=2 * tokens * width * depth,
            bytes_accessed=2 * tokens * (width + depth) + 4 * width * depth,
            transcendentals=0,
        ),
    )(input_whole.reshape(16, 2, half, width), grad_blocks, grad_other)


def local(layer_input, weight, gelu_input, upstream):
    tokens, width = layer_input.shape
    half = tokens // 2
    f32, bf16 = jnp.float32, jnp.bfloat16

    input_whole = lax.all_gather(layer_input, "col", axis=0, tiled=True)
    gelu_grad = (upstream.astype(f32) * gelu_slope(gelu_input.astype(f32))).astype(bf16)

    both, blocks = (2, half, 2 * width), (16, half, gelu_grad.shape[1])
    shapes = (((2,) + both, bf16), (both, f32), (both, f32), (blocks, bf16), (blocks, bf16))
    to_send, middle, here, grad_blocks, grad_other = lax.cond(
        lax.axis_index("col") < 16,
        first_round,
        lambda g, w: tuple(jnp.zeros(*v) for v in shapes),
        gelu_grad,
        weight,
    )

    moved = send(to_send, 2)
    grad_weight = weight_gradient(input_whole, grad_blocks, grad_other)
    moved, grad_weight = lax.optimization_barrier((moved, grad_weight))
    part = (2, half, width)
    outs = [jax.ShapeDtypeStruct(part, t) for t in (bf16, bf16, f32, bf16)]
    own, cross, stay, swapped = call(second_kernel, outs, (moved, middle, here))
    last = send(own, 4), send(cross, 4, cross=True), stay, swap_cores(swapped)
    outs = [jax.ShapeDtypeStruct((tokens, width), bf16)]
    grad_input = call(third_kernel, outs, last)[0]
    return (grad_input, grad_weight)


def solution(mesh):
    in_specs = (
        P("col", ("row", "rep")),
        P(("row", "rep"), "col"),
        P(("row", "rep"), "col"),
        P(("row", "rep"), "col"),
    )
    out_specs = (P("col", ("row", "rep")), P(("row", "rep"), "col"))
    return jax.shard_map(local, mesh=mesh, in_specs=in_specs, out_specs=out_specs, check_vma=False)
```

```python
import functools
import math

import jax
import jax.numpy as jnp
from jax import lax
from jax.experimental import pallas as pl
from jax.experimental.pallas import tpu as pltpu
from jax.sharding import PartitionSpec as P

cubic_term = 0.044715
plane = ("row", "rep")
ring = ("col", "rep")


def gelu_slope(values):
    scale = math.sqrt(2.0 / math.pi)
    inner = scale * (values + cubic_term * values * values * values)
    tangent = jnp.tanh(inner)
    return 0.5 * (1.0 + tangent) + 0.5 * values * (1.0 - tangent * tangent) * scale * (
        1.0 + 3.0 * cubic_term * values * values
    )


def index(x, y, core):
    return ((x * 2 + y % 2) * 2 + y // 2) * 2 + core


y_order = (0, 2, 1, 3)
along_x = [[[index(x, y, core) for x in range(4)] for y in y_order] for core in range(2)]
along_y = [[[index(x, y, core) for y in y_order] for x in range(4)] for core in range(2)]


first_groups = (((8,), False), ((7, 5, 3, 1), False))
early_groups = (((-7, -5, -3, -1), True),)
late_groups = (((6, 4, 2, 0), False), ((-6, -4, -2), True))


def place(step):
    core = lax.rem(lax.axis_index("rep"), 2)
    chip = lax.rem(lax.axis_index("col") + (1 - 2 * core) * step + 16, 16)
    return jnp.where(core == 0, lax.rem(chip, 4) * 4 + lax.div(chip, 4), chip)


def gather(values, groups):
    copies = jnp.broadcast_to(values[None], (4,) + values.shape)
    parts = lax.all_to_all(copies, plane, 0, 0, axis_index_groups=groups)
    return parts.reshape((4 * values.shape[0],) + values.shape[1:])


def swap_cores(values):
    return lax.ppermute(values, "rep", [(0, 1), (1, 0), (2, 3), (3, 2)])


def send(values, distance, cross=False):
    pairs = []
    for z in range(16):
        for rep in range(4):
            target = (z + (-distance if rep % 2 else distance)) % 16
            pairs.append((z * 4 + rep, target * 4 + (rep ^ 1 if cross else rep)))
    return lax.ppermute(values, ring, pairs)


def matmul_nt(a, b):
    return lax.dot_general(a, b, (((1,), (1,)), ((), ())), preferred_element_type=jnp.float32)


def matmul_tn(a, b):
    return lax.dot_general(a, b, (((0,), (0,)), ((), ())), preferred_element_type=jnp.float32)


def call(kernel, outs, args, flops=0, scratch=()):
    vmem = pl.BlockSpec(memory_space=pltpu.VMEM)
    moved = sum(v.size * v.dtype.itemsize for v in tuple(args) + tuple(outs))
    return pl.pallas_call(
        kernel,
        out_shape=outs,
        in_specs=[vmem] * len(args),
        out_specs=tuple(vmem for _ in outs),
        scratch_shapes=scratch,
        compiler_params=pltpu.CompilerParams(vmem_limit_bytes=32 * 1024 * 1024),
        cost_estimate=pl.CostEstimate(flops=flops, bytes_accessed=moved, transcendentals=0),
    )(*args)


def partial_kernel(groups, add, grad_ref, own_ref, other_ref, *refs):
    width = own_ref.shape[0]
    first_ref, outs = (refs[0], refs[1:]) if add else (None, refs)
    for (steps, flipped), out_ref in zip(groups, outs):
        rows = jnp.concatenate([grad_ref[place(step)] for step in steps], axis=0)
        for side, ref in enumerate((other_ref, own_ref) if flipped else (own_ref, other_ref)):
            part = matmul_nt(rows, ref[...]).reshape(len(steps), -1, width)
            columns = slice(side * width, (side + 1) * width)
            out_ref[:, :, columns] = part.astype(out_ref.dtype)
            if first_ref is not None and out_ref is outs[0]:
                first = part[0] + first_ref[0, :, columns].astype(jnp.float32)
                out_ref[0, :, columns] = first.astype(out_ref.dtype)


def partials(groups, grad_blocks, weight_own, weight_other, *add):
    rows, depth = grad_blocks.shape[1:]
    width = weight_own.shape[0]
    outs = [jax.ShapeDtypeStruct((len(g[0]), rows, 2 * width), jnp.bfloat16) for g in groups]
    return call(
        functools.partial(partial_kernel, groups, bool(add)),
        outs,
        (grad_blocks, weight_own, weight_other, *add),
        flops=4 * sum(len(g[0]) for g in groups) * rows * depth * width,
    )


def first_kernel(own_ref, cross_ref, rest_ref, other_ref, send_ref, middle_ref, here_ref):
    def total(i, *refs):
        return sum(ref[i].astype(jnp.float32) for ref in refs)

    dtype = send_ref.dtype
    send_ref[0, 0] = total(0, own_ref, rest_ref).astype(dtype)
    send_ref[0, 1] = total(0, cross_ref, other_ref).astype(dtype)
    send_ref[1, 0] = total(2, own_ref, rest_ref).astype(dtype)
    send_ref[1, 1] = total(2, cross_ref, other_ref).astype(dtype)
    middle_ref[0] = total(1, own_ref, rest_ref)
    middle_ref[1] = total(1, cross_ref, other_ref)
    here_ref[0] = total(3, own_ref, rest_ref)
    here_ref[1] = total(3, cross_ref)


def second_kernel(moved_ref, middle_ref, here_ref, own_ref, cross_ref, stay_ref, swap_ref):
    width = own_ref.shape[2]
    ahead = (middle_ref[...] + moved_ref[0].astype(jnp.float32)).astype(own_ref.dtype)
    own_ref[...] = ahead[:, :, :width]
    cross_ref[...] = ahead[:, :, width:]
    here = here_ref[...] + moved_ref[1].astype(jnp.float32)
    stay_ref[...] = here[:, :, :width]
    swap_ref[...] = here[:, :, width:].astype(swap_ref.dtype)


def third_kernel(own_ref, cross_ref, stay_ref, swap_ref, out_ref):
    half = own_ref.shape[1]
    core = lax.rem(lax.axis_index("rep"), 2)
    for i, place_of in enumerate((core, 1 - core)):
        other = cross_ref[1 - i].astype(jnp.float32) + swap_ref[1 - i].astype(jnp.float32)
        part = stay_ref[i] + own_ref[i].astype(jnp.float32) + other
        rows = pl.ds(pl.multiple_of(place_of * half, half), half)
        out_ref[rows, :] = part.astype(out_ref.dtype)


def taken(step, *args):
    return lax.cond(
        lax.axis_index("col") < 16,
        step,
        lambda *a: jax.tree.map(lambda v: jnp.zeros(v.shape, v.dtype), jax.eval_shape(step, *a)),
        *args,
    )


def first_round(grad_blocks, weight, weight_other):
    far, ahead = partials(first_groups, grad_blocks, weight, weight_other)
    far = send(far, 2)
    own = send(ahead, 1)
    ahead, next_blocks = lax.optimization_barrier((ahead, grad_blocks))
    behind = partials(early_groups, next_blocks, weight, weight_other)[0]
    cross = send(behind, -1, cross=True)
    behind, later_blocks = lax.optimization_barrier((behind, next_blocks))
    rest, for_sibling = partials(late_groups, later_blocks, weight, weight_other, far)
    rest_sibling = swap_cores(for_sibling)

    both = (2,) + rest.shape[1:]
    outs = [
        jax.ShapeDtypeStruct((2,) + both, jnp.bfloat16),
        jax.ShapeDtypeStruct(both, jnp.float32),
        jax.ShapeDtypeStruct(both, jnp.float32),
    ]
    return call(first_kernel, outs, (own, cross, rest, rest_sibling))


def gather_plane(gelu_grad, weight):
    line = gather(gelu_grad, along_x[0] + along_y[1])
    grad_tokens = gather(line, along_y[0] + along_x[1])
    return grad_tokens.reshape((16,) + gelu_grad.shape), swap_cores(weight)


def gather_and_round(gelu_grad, weight):
    grad_blocks, weight_other = taken(gather_plane, gelu_grad, weight)
    grad_other = swap_cores(grad_blocks)
    return (*taken(first_round, grad_blocks, weight, weight_other), grad_blocks, grad_other)


def weight_kernel(sibling, input_ref, grad_ref, *refs):
    first_ref = refs[0] if len(refs) == 3 else None
    out_ref, rows_ref = refs[-2:]
    half, depth = grad_ref.shape[1:]
    core = lax.rem(lax.axis_index("rep"), 2)
    core = 1 - core if sibling else core
    for chip in range(16):
        at = jnp.where(core == 0, (chip % 4) * 4 + chip // 4, chip)
        rows = pl.ds(pl.multiple_of(at * half, half), half)
        rows_ref[rows, :] = input_ref[chip, core]
    tile = 256
    for start in range(0, depth, tile):
        grad = grad_ref[:, :, start : start + tile].reshape(16 * half, tile)
        part = matmul_tn(rows_ref[...], grad)
        if first_ref is not None:
            part = part + first_ref[:, start : start + tile]
        out_ref[:, start : start + tile] = part


def weight_gradient(sibling, input_whole, grad_blocks, *first):
    tokens, width = input_whole.shape
    half, depth = grad_blocks.shape[1:]
    out = jax.ShapeDtypeStruct((width, depth), jnp.float32)
    return call(
        functools.partial(weight_kernel, sibling),
        [out],
        (input_whole.reshape(16, 2, half, width), grad_blocks, *first),
        flops=tokens * width * depth,
        scratch=[pltpu.VMEM((tokens // 2, width), jnp.bfloat16)],
    )[0]


def local(layer_input, weight, gelu_input, upstream):
    tokens, width = layer_input.shape
    half = tokens // 2
    f32, bf16 = jnp.float32, jnp.bfloat16

    input_whole = lax.all_gather(layer_input, "col", axis=0, tiled=True)
    gelu_grad = (upstream.astype(f32) * gelu_slope(gelu_input.astype(f32))).astype(bf16)

    to_send, middle, here, grad_blocks, grad_other = taken(gather_and_round, gelu_grad, weight)

    moved = send(to_send, 2)
    grad_weight = weight_gradient(False, input_whole, grad_blocks)
    grad_weight = weight_gradient(True, input_whole, grad_other, grad_weight)
    moved, grad_weight = lax.optimization_barrier((moved, grad_weight))
    part = (2, half, width)
    outs = [jax.ShapeDtypeStruct(part, t) for t in (bf16, bf16, f32, bf16)]
    own, cross, stay, swapped = call(second_kernel, outs, (moved, middle, here))
    last = send(own, 4), send(cross, 4, cross=True), stay, swap_cores(swapped)
    outs = [jax.ShapeDtypeStruct((tokens, width), bf16)]
    grad_input = call(third_kernel, outs, last)[0]
    return (grad_input, grad_weight)


def solution(mesh):
    in_specs = (
        P("col", ("row", "rep")),
        P(("row", "rep"), "col"),
        P(("row", "rep"), "col"),
        P(("row", "rep"), "col"),
    )
    out_specs = (P("col", ("row", "rep")), P(("row", "rep"), "col"))
    return jax.shard_map(local, mesh=mesh, in_specs=in_specs, out_specs=out_specs, check_vma=False)
```

```python
import functools
import math

import jax
import jax.numpy as jnp
from jax import lax
from jax.experimental import pallas as pl
from jax.experimental.pallas import tpu as pltpu
from jax.sharding import PartitionSpec as P

cubic_term = 0.044715
plane = ("row", "rep")
ring = ("col", "rep")


def gelu_slope(values):
    scale = math.sqrt(2.0 / math.pi)
    inner = scale * (values + cubic_term * values * values * values)
    tangent = jnp.tanh(inner)
    return 0.5 * (1.0 + tangent) + 0.5 * values * (1.0 - tangent * tangent) * scale * (
        1.0 + 3.0 * cubic_term * values * values
    )


def index(x, y, core):
    return ((x * 2 + y % 2) * 2 + y // 2) * 2 + core


y_order = (0, 2, 1, 3)
along_x = [[[index(x, y, core) for x in range(4)] for y in y_order] for core in range(2)]
along_y = [[[index(x, y, core) for y in y_order] for x in range(4)] for core in range(2)]


early_groups = (
    (((8, 0),), False),
    (((7, 0), (5, 0), (3, 0), (1, 0)), False),
    (((-7, 0), (-5, 0), (-3, 0), (-1, 0)), True),
)
late_groups = (
    (((6, 0), (4, 0), (2, 0), (0, 0)), False),
    (((6, 1), (4, 1), (2, 1)), False),
)


def place(chip, core):
    turned = lax.rem(chip, 4) * 4 + lax.div(chip, 4)
    return jnp.where(core == 0, turned, chip)


def gather(values, groups):
    copies = jnp.broadcast_to(values[None], (4,) + values.shape)
    parts = lax.all_to_all(copies, plane, 0, 0, axis_index_groups=groups)
    return parts.reshape((4 * values.shape[0],) + values.shape[1:])


def swap_cores(values):
    return lax.ppermute(values, "rep", [(0, 1), (1, 0), (2, 3), (3, 2)])


def send(values, distance, cross=False):
    pairs = []
    for z in range(16):
        for rep in range(4):
            target = (z + (-distance if rep % 2 else distance)) % 16
            pairs.append((z * 4 + rep, target * 4 + (rep ^ 1 if cross else rep)))
    return lax.ppermute(values, ring, pairs)


def matmul_nt(a, b):
    return lax.dot_general(a, b, (((1,), (1,)), ((), ())), preferred_element_type=jnp.float32)


def matmul_tn(a, b):
    return lax.dot_general(a, b, (((0,), (0,)), ((), ())), preferred_element_type=jnp.float32)


def call(kernel, outs, args, flops=0, scratch=(), space=pltpu.VMEM, out_space=pltpu.VMEM):
    moved = sum(v.size * v.dtype.itemsize for v in tuple(args) + tuple(outs))
    return pl.pallas_call(
        kernel,
        out_shape=outs,
        in_specs=[pl.BlockSpec(memory_space=space) for _ in args],
        out_specs=tuple(pl.BlockSpec(memory_space=out_space) for _ in outs),
        scratch_shapes=scratch,
        compiler_params=pltpu.CompilerParams(vmem_limit_bytes=40 * 1024 * 1024),
        cost_estimate=pl.CostEstimate(flops=flops, bytes_accessed=moved, transcendentals=0),
    )(*args)


def partial_kernel(groups, n_grads, n_in, *refs):
    grad_refs, weight_refs = refs[:n_grads], refs[n_grads : n_grads + 2]
    add_refs = refs[n_grads + 2 : n_in]
    outs = refs[n_in : n_in + len(groups)]
    blocks_ref, weights_ref, add_ref, block_sems, weight_sems, add_sem = refs[n_in + len(groups) :]
    core = lax.rem(lax.axis_index("rep"), 2)
    z = lax.axis_index("col")
    width = weights_ref.shape[1]

    weight_copies = [
        pltpu.make_async_copy(ref, weights_ref.at[i], weight_sems.at[i])
        for i, ref in enumerate(weight_refs)
    ]
    block_copies = []
    for items, _ in groups:
        for step, whose in items:
            chip = lax.rem(z + (1 - 2 * core) * step + 16, 16)
            at = place(chip, 1 - core if whose else core)
            i = len(block_copies)
            block_copies.append(
                pltpu.make_async_copy(grad_refs[whose].at[at], blocks_ref.at[i], block_sems.at[i])
            )
    add_copies = [pltpu.make_async_copy(ref, add_ref, add_sem) for ref in add_refs]
    for copy in weight_copies[:1] + block_copies + weight_copies[1:] + add_copies:
        copy.start()

    start = 0
    for number, ((items, flipped), out_ref) in enumerate(zip(groups, outs)):
        count = len(items)
        for copy in block_copies[start : start + count]:
            copy.wait()
        rows = blocks_ref[start : start + count].reshape(count * blocks_ref.shape[1], -1)
        start += count
        for side in range(2):
            if number == 0:
                weight_copies[side].wait()
            part = matmul_nt(rows, weights_ref[side]).reshape(count, -1, width)
            at = (1 - side if flipped else side) * width
            columns = slice(at, at + width)
            out_ref[:, :, columns] = part.astype(out_ref.dtype)
            if add_copies and number == 0:
                if side == 0:
                    add_copies[0].wait()
                first = part[0] + add_ref[0, :, columns].astype(jnp.float32)
                out_ref[0, :, columns] = first.astype(out_ref.dtype)


def partials(groups, grads, weights, *add):
    rows, depth = grads[0].shape[1:]
    width = weights[0].shape[0]
    count = sum(len(items) for items, _ in groups)
    bf16 = jnp.bfloat16
    args = (*grads, *weights, *add)
    return call(
        functools.partial(partial_kernel, groups, len(grads), len(args)),
        [jax.ShapeDtypeStruct((len(items), rows, 2 * width), bf16) for items, _ in groups],
        args,
        flops=4 * count * rows * depth * width,
        scratch=[
            pltpu.VMEM((count, rows, depth), bf16),
            pltpu.VMEM((2, width, depth), bf16),
            pltpu.VMEM((1, rows, 2 * width), bf16),
            pltpu.SemaphoreType.DMA((count,)),
            pltpu.SemaphoreType.DMA((2,)),
            pltpu.SemaphoreType.DMA,
        ],
        space=pl.ANY,
    )


def first_kernel(own_ref, cross_ref, rest_ref, other_ref, send_ref, middle_ref, here_ref):
    def total(i, *refs):
        return sum(ref[i].astype(jnp.float32) for ref in refs)

    dtype = send_ref.dtype
    send_ref[0, 0] = total(0, own_ref, rest_ref).astype(dtype)
    send_ref[0, 1] = total(0, cross_ref, other_ref).astype(dtype)
    send_ref[1, 0] = total(2, own_ref, rest_ref).astype(dtype)
    send_ref[1, 1] = total(2, cross_ref, other_ref).astype(dtype)
    middle_ref[0] = total(1, own_ref, rest_ref)
    middle_ref[1] = total(1, cross_ref, other_ref)
    here_ref[0] = total(3, own_ref, rest_ref)
    here_ref[1] = total(3, cross_ref)


def second_kernel(moved_ref, middle_ref, here_ref, own_ref, cross_ref, stay_ref, swap_ref):
    width = own_ref.shape[2]
    ahead = (middle_ref[...] + moved_ref[0].astype(jnp.float32)).astype(own_ref.dtype)
    own_ref[...] = ahead[:, :, :width]
    cross_ref[...] = ahead[:, :, width:]
    here = here_ref[...] + moved_ref[1].astype(jnp.float32)
    stay_ref[...] = here[:, :, :width]
    swap_ref[...] = here[:, :, width:].astype(swap_ref.dtype)


def third_kernel(own_ref, cross_ref, stay_ref, swap_ref, out_ref):
    half = own_ref.shape[1]
    core = lax.rem(lax.axis_index("rep"), 2)
    for i, place_of in enumerate((core, 1 - core)):
        other = cross_ref[1 - i].astype(jnp.float32) + swap_ref[1 - i].astype(jnp.float32)
        part = stay_ref[i] + own_ref[i].astype(jnp.float32) + other
        rows = pl.ds(pl.multiple_of(place_of * half, half), half)
        out_ref[rows, :] = part.astype(out_ref.dtype)


def taken(step, *args):
    return lax.cond(
        lax.axis_index("col") < 16,
        step,
        lambda *a: jax.tree.map(lambda v: jnp.zeros(v.shape, v.dtype), jax.eval_shape(step, *a)),
        *args,
    )


def first_round(grad_blocks, weight, weight_other):
    grad_other = swap_cores(grad_blocks)
    weights = weight, weight_other
    far, ahead, behind = partials(early_groups, (grad_blocks,), weights)
    far = send(far, 2)
    own, cross = send(ahead, 1), send(behind, -1, cross=True)
    rest, rest_other = partials(late_groups, (grad_blocks, grad_other), weights, far)

    both = (2,) + rest.shape[1:]
    outs = [
        jax.ShapeDtypeStruct((2,) + both, jnp.bfloat16),
        jax.ShapeDtypeStruct(both, jnp.float32),
        jax.ShapeDtypeStruct(both, jnp.float32),
    ]
    return (*call(first_kernel, outs, (own, cross, rest, rest_other)), grad_other)


def gather_plane(gelu_grad, weight):
    line = gather(gelu_grad, along_x[0] + along_y[1])
    grad_tokens = gather(line, along_y[0] + along_x[1])
    return grad_tokens.reshape((16,) + gelu_grad.shape), swap_cores(weight)


def gather_and_round(gelu_grad, weight):
    grad_blocks, weight_other = taken(gather_plane, gelu_grad, weight)
    return (*taken(first_round, grad_blocks, weight, weight_other), grad_blocks)


def weight_kernel(input_ref, *refs):
    grad_refs, out_ref = refs[:2], refs[2]
    rows_ref, grads_ref, parts_ref, row_sems, grad_sems, out_sems = refs[3:]
    half, tiles, tile = input_ref.shape[2], grads_ref.shape[1], grads_ref.shape[4]
    core = lax.rem(lax.axis_index("rep"), 2)
    row_copies, grad_copies, out_copies = [], [], []
    for whose in range(2):
        holder = 1 - core if whose else core
        for chip in range(16):
            at = jnp.where(holder == 0, (chip % 4) * 4 + chip // 4, chip)
            rows = pl.ds(pl.multiple_of(at * half, half), half)
            row_copies.append(
                pltpu.make_async_copy(
                    input_ref.at[chip, holder],
                    rows_ref.at[whose, rows],
                    row_sems.at[whose * 16 + chip],
                )
            )
    for i in range(tiles):
        columns = pl.ds(i * tile, tile)
        for whose, ref in enumerate(grad_refs):
            grad_copies.append(
                pltpu.make_async_copy(
                    ref.at[:, :, columns], grads_ref.at[whose, i], grad_sems.at[2 * i + whose]
                )
            )
        out_copies.append(
            pltpu.make_async_copy(parts_ref.at[i], out_ref.at[:, columns], out_sems.at[i])
        )
    for copy in row_copies + grad_copies:
        copy.start()
    for copy in row_copies:
        copy.wait()
    for i in range(tiles):
        part = None
        for whose in range(2):
            grad_copies[2 * i + whose].wait()
            grad = grads_ref[whose, i].reshape(16 * half, tile)
            product = matmul_tn(rows_ref[whose], grad)
            part = product if part is None else part + product
        parts_ref[i] = part
        out_copies[i].start()
    for copy in out_copies:
        copy.wait()


def weight_gradient(input_whole, grad_blocks, grad_other):
    tokens, width = input_whole.shape
    half, depth = grad_blocks.shape[1:]
    tile = 256
    tiles = depth // tile
    bf16 = jnp.bfloat16
    return call(
        weight_kernel,
        [jax.ShapeDtypeStruct((width, depth), jnp.float32)],
        (input_whole.reshape(16, 2, half, width), grad_blocks, grad_other),
        flops=2 * tokens * width * depth,
        scratch=[
            pltpu.VMEM((2, tokens // 2, width), bf16),
            pltpu.VMEM((2, tiles, 16, half, tile), bf16),
            pltpu.VMEM((tiles, width, tile), jnp.float32),
            pltpu.SemaphoreType.DMA((32,)),
            pltpu.SemaphoreType.DMA((2 * tiles,)),
            pltpu.SemaphoreType.DMA((tiles,)),
        ],
        space=pl.ANY,
        out_space=pl.ANY,
    )[0]


def local(layer_input, weight, gelu_input, upstream):
    tokens, width = layer_input.shape
    half = tokens // 2
    f32, bf16 = jnp.float32, jnp.bfloat16

    input_whole = lax.all_gather(layer_input, "col", axis=0, tiled=True)
    gelu_grad = (upstream.astype(f32) * gelu_slope(gelu_input.astype(f32))).astype(bf16)

    to_send, middle, here, grad_other, grad_blocks = taken(gather_and_round, gelu_grad, weight)

    moved = send(to_send, 2)
    grad_weight = weight_gradient(input_whole, grad_blocks, grad_other)
    moved, grad_weight = lax.optimization_barrier((moved, grad_weight))
    part = (2, half, width)
    outs = [jax.ShapeDtypeStruct(part, t) for t in (bf16, bf16, f32, bf16)]
    own, cross, stay, swapped = call(second_kernel, outs, (moved, middle, here))
    last = send(own, 4), send(cross, 4, cross=True), stay, swap_cores(swapped)
    outs = [jax.ShapeDtypeStruct((tokens, width), bf16)]
    grad_input = call(third_kernel, outs, last)[0]
    return (grad_input, grad_weight)


def solution(mesh):
    in_specs = (
        P("col", ("row", "rep")),
        P(("row", "rep"), "col"),
        P(("row", "rep"), "col"),
        P(("row", "rep"), "col"),
    )
    out_specs = (P("col", ("row", "rep")), P(("row", "rep"), "col"))
    return jax.shard_map(local, mesh=mesh, in_specs=in_specs, out_specs=out_specs, check_vma=False)
```

```python
import functools
import math

import jax
import jax.numpy as jnp
from jax import lax
from jax.experimental import pallas as pl
from jax.experimental.pallas import tpu as pltpu
from jax.sharding import PartitionSpec as P

cubic_term = 0.044715
plane = ("row", "rep")
ring = ("col", "rep")


def gelu_slope(values):
    scale = math.sqrt(2.0 / math.pi)
    inner = scale * (values + cubic_term * values * values * values)
    tangent = jnp.tanh(inner)
    return 0.5 * (1.0 + tangent) + 0.5 * values * (1.0 - tangent * tangent) * scale * (
        1.0 + 3.0 * cubic_term * values * values
    )


def index(x, y, core):
    return ((x * 2 + y % 2) * 2 + y // 2) * 2 + core


y_order = (0, 2, 1, 3)
along_x = [[[index(x, y, core) for x in range(4)] for y in y_order] for core in range(2)]
along_y = [[[index(x, y, core) for y in y_order] for x in range(4)] for core in range(2)]


early_groups = (((8,), False), ((7, 5, 3, 1), False), ((-7, -5, -3, -1), True))
late_groups = (((6, 4, 2, 0), False), ((-6, -4, -2), True))


def place(chip, core):
    turned = lax.rem(chip, 4) * 4 + lax.div(chip, 4)
    return jnp.where(core == 0, turned, chip)


def gather(values, groups):
    copies = jnp.broadcast_to(values[None], (4,) + values.shape)
    parts = lax.all_to_all(copies, plane, 0, 0, axis_index_groups=groups)
    return parts.reshape((4 * values.shape[0],) + values.shape[1:])


def swap_cores(values):
    return lax.ppermute(values, "rep", [(0, 1), (1, 0), (2, 3), (3, 2)])


def send(values, distance, cross=False):
    pairs = []
    for z in range(16):
        for rep in range(4):
            target = (z + (-distance if rep % 2 else distance)) % 16
            pairs.append((z * 4 + rep, target * 4 + (rep ^ 1 if cross else rep)))
    return lax.ppermute(values, ring, pairs)


def matmul_nt(a, b):
    return lax.dot_general(a, b, (((1,), (1,)), ((), ())), preferred_element_type=jnp.float32)


def matmul_tn(a, b):
    return lax.dot_general(a, b, (((0,), (0,)), ((), ())), preferred_element_type=jnp.float32)


def call(kernel, outs, args, flops=0, scratch=()):
    vmem = pl.BlockSpec(memory_space=pltpu.VMEM)
    moved = sum(v.size * v.dtype.itemsize for v in tuple(args) + tuple(outs))
    return pl.pallas_call(
        kernel,
        out_shape=outs,
        in_specs=[vmem] * len(args),
        out_specs=tuple(vmem for _ in outs),
        scratch_shapes=scratch,
        compiler_params=pltpu.CompilerParams(vmem_limit_bytes=40 * 1024 * 1024),
        cost_estimate=pl.CostEstimate(flops=flops, bytes_accessed=moved, transcendentals=0),
    )(*args)


def partial_kernel(groups, dots, grad_ref, own_ref, other_ref, *refs):
    outs = refs[-len(groups) :]
    add_ref = refs[0] if len(refs) > len(groups) else None
    core = lax.rem(lax.axis_index("rep"), 2)
    z = lax.axis_index("col")
    width = own_ref.shape[0]
    blocks = [
        (out_ref, i, flipped, lax.rem(z + (1 - 2 * core) * step + 16, 16))
        for (steps, flipped), out_ref in zip(groups, outs)
        for i, step in enumerate(steps)
    ]
    start = 0
    for count in dots:
        taken_now = blocks[start : start + count]
        rows = jnp.concatenate([grad_ref[place(chip, core)] for _, _, _, chip in taken_now], axis=0)
        for side, ref in enumerate((own_ref, other_ref)):
            part = matmul_nt(rows, ref[...]).reshape(count, -1, width)
            for j, (out_ref, i, flipped, _) in enumerate(taken_now):
                at = (1 - side if flipped else side) * width
                value = part[j]
                if add_ref is not None and start + j == 0:
                    value = value + add_ref[0, :, at : at + width].astype(jnp.float32)
                out_ref[i, :, at : at + width] = value.astype(out_ref.dtype)
        start += count


def partials(groups, dots, grad_blocks, weights, *add):
    rows, depth = grad_blocks.shape[1:]
    width = weights[0].shape[0]
    return call(
        functools.partial(partial_kernel, groups, dots),
        [jax.ShapeDtypeStruct((len(g[0]), rows, 2 * width), jnp.bfloat16) for g in groups],
        (grad_blocks, *weights, *add),
        flops=12 * sum(dots) * rows * depth * width,
    )


def first_kernel(own_ref, cross_ref, rest_ref, other_ref, send_ref, middle_ref, here_ref):
    def total(i, *refs):
        return sum(ref[i].astype(jnp.float32) for ref in refs)

    dtype = send_ref.dtype
    send_ref[0, 0] = total(0, own_ref, rest_ref).astype(dtype)
    send_ref[0, 1] = total(0, cross_ref, other_ref).astype(dtype)
    send_ref[1, 0] = total(2, own_ref, rest_ref).astype(dtype)
    send_ref[1, 1] = total(2, cross_ref, other_ref).astype(dtype)
    middle_ref[0] = total(1, own_ref, rest_ref)
    middle_ref[1] = total(1, cross_ref, other_ref)
    here_ref[0] = total(3, own_ref, rest_ref)
    here_ref[1] = total(3, cross_ref)


def second_kernel(moved_ref, middle_ref, here_ref, own_ref, cross_ref, stay_ref, swap_ref):
    width = own_ref.shape[2]
    ahead = (middle_ref[...] + moved_ref[0].astype(jnp.float32)).astype(own_ref.dtype)
    own_ref[...] = ahead[:, :, :width]
    cross_ref[...] = ahead[:, :, width:]
    here = here_ref[...] + moved_ref[1].astype(jnp.float32)
    stay_ref[...] = here[:, :, :width]
    swap_ref[...] = here[:, :, width:].astype(swap_ref.dtype)


def third_kernel(own_ref, cross_ref, stay_ref, swap_ref, out_ref):
    half = own_ref.shape[1]
    core = lax.rem(lax.axis_index("rep"), 2)
    for i, place_of in enumerate((core, 1 - core)):
        other = cross_ref[1 - i].astype(jnp.float32) + swap_ref[1 - i].astype(jnp.float32)
        part = stay_ref[i] + own_ref[i].astype(jnp.float32) + other
        rows = pl.ds(pl.multiple_of(place_of * half, half), half)
        out_ref[rows, :] = part.astype(out_ref.dtype)


def taken(step, *args):
    return lax.cond(
        lax.axis_index("col") < 16,
        step,
        lambda *a: jax.tree.map(lambda v: jnp.zeros(v.shape, v.dtype), jax.eval_shape(step, *a)),
        *args,
    )


def first_round(grad_blocks, weight, weight_other):
    weights = weight, weight_other
    far, ahead, behind = partials(early_groups, (5, 4), grad_blocks, weights)
    far, later_blocks = lax.optimization_barrier((far, grad_blocks))
    far = send(far, 2)
    own, cross = send(ahead, 1), send(behind, -1, cross=True)
    rest, for_sibling = partials(late_groups, (7,), later_blocks, weights, far)
    rest_other = swap_cores(for_sibling)

    both = (2,) + rest.shape[1:]
    outs = [
        jax.ShapeDtypeStruct((2,) + both, jnp.bfloat16),
        jax.ShapeDtypeStruct(both, jnp.float32),
        jax.ShapeDtypeStruct(both, jnp.float32),
    ]
    return call(first_kernel, outs, (own, cross, rest, rest_other))


def gather_plane(gelu_grad, weight):
    line = gather(gelu_grad, along_x[0] + along_y[1])
    grad_tokens = gather(line, along_y[0] + along_x[1])
    return grad_tokens.reshape((16,) + gelu_grad.shape), swap_cores(weight)


def gather_and_round(gelu_grad, weight):
    grad_blocks, weight_other = taken(gather_plane, gelu_grad, weight)
    return (*taken(first_round, grad_blocks, weight, weight_other), grad_blocks)


def weight_kernel(sibling, input_ref, grad_ref, *refs):
    first_ref = refs[0] if len(refs) == 3 else None
    out_ref, rows_ref = refs[-2:]
    half, depth = grad_ref.shape[1:]
    core = lax.rem(lax.axis_index("rep"), 2)
    core = 1 - core if sibling else core
    for chip in range(16):
        at = jnp.where(core == 0, (chip % 4) * 4 + chip // 4, chip)
        rows = pl.ds(pl.multiple_of(at * half, half), half)
        rows_ref[rows, :] = input_ref[chip, core]
    tile = 256
    for start in range(0, depth, tile):
        grad = grad_ref[:, :, start : start + tile].reshape(16 * half, tile)
        part = matmul_tn(rows_ref[...], grad)
        if first_ref is not None:
            part = part + first_ref[:, start : start + tile]
        out_ref[:, start : start + tile] = part


def weight_gradient(sibling, input_whole, grad_blocks, *first):
    tokens, width = input_whole.shape
    half, depth = grad_blocks.shape[1:]
    out = jax.ShapeDtypeStruct((width, depth), jnp.float32)
    return call(
        functools.partial(weight_kernel, sibling),
        [out],
        (input_whole.reshape(16, 2, half, width), grad_blocks, *first),
        flops=(1 if sibling else 40) * tokens * width * depth,
        scratch=[pltpu.VMEM((tokens // 2, width), jnp.bfloat16)],
    )[0]


def local(layer_input, weight, gelu_input, upstream):
    tokens, width = layer_input.shape
    half = tokens // 2
    f32, bf16 = jnp.float32, jnp.bfloat16

    input_whole = lax.all_gather(layer_input, "col", axis=0, tiled=True)
    gelu_grad = (upstream.astype(f32) * gelu_slope(gelu_input.astype(f32))).astype(bf16)

    to_send, middle, here, grad_blocks = taken(gather_and_round, gelu_grad, weight)

    moved = send(to_send, 2)
    grad_other = swap_cores(grad_blocks)
    grad_weight = weight_gradient(False, input_whole, grad_blocks)
    grad_weight = weight_gradient(True, input_whole, grad_other, grad_weight)
    moved, grad_weight = lax.optimization_barrier((moved, grad_weight))
    part = (2, half, width)
    outs = [jax.ShapeDtypeStruct(part, t) for t in (bf16, bf16, f32, bf16)]
    own, cross, stay, swapped = call(second_kernel, outs, (moved, middle, here))
    last = send(own, 4), send(cross, 4, cross=True), stay, swap_cores(swapped)
    outs = [jax.ShapeDtypeStruct((tokens, width), bf16)]
    grad_input = call(third_kernel, outs, last)[0]
    return (grad_input, grad_weight)


def solution(mesh):
    in_specs = (
        P("col", ("row", "rep")),
        P(("row", "rep"), "col"),
        P(("row", "rep"), "col"),
        P(("row", "rep"), "col"),
    )
    out_specs = (P("col", ("row", "rep")), P(("row", "rep"), "col"))
    return jax.shard_map(local, mesh=mesh, in_specs=in_specs, out_specs=out_specs, check_vma=False)
```

```python
import functools
import math

import jax
import jax.numpy as jnp
from jax import lax
from jax.experimental import pallas as pl
from jax.experimental.pallas import tpu as pltpu
from jax.sharding import PartitionSpec as P

cubic_term = 0.044715
plane = ("row", "rep")
ring = ("col", "rep")


def gelu_slope(values):
    scale = math.sqrt(2.0 / math.pi)
    inner = scale * (values + cubic_term * values * values * values)
    tangent = jnp.tanh(inner)
    return 0.5 * (1.0 + tangent) + 0.5 * values * (1.0 - tangent * tangent) * scale * (
        1.0 + 3.0 * cubic_term * values * values
    )


def index(x, y, core):
    return ((x * 2 + y % 2) * 2 + y // 2) * 2 + core


y_order = (0, 2, 1, 3)
along_x = [[[index(x, y, core) for x in range(4)] for y in y_order] for core in range(2)]
along_y = [[[index(x, y, core) for y in y_order] for x in range(4)] for core in range(2)]


first_groups = (((8,), False), ((7, 5, 3, 1), False))
early_groups = (((-7, -5, -3, -1), True),)
late_groups = (((6, 4, 2, 0), False), ((-6, -4, -2), True))


def place(chip, core):
    turned = lax.rem(chip, 4) * 4 + lax.div(chip, 4)
    return jnp.where(core == 0, turned, chip)


def gather(values, groups):
    copies = jnp.broadcast_to(values[None], (4,) + values.shape)
    parts = lax.all_to_all(copies, plane, 0, 0, axis_index_groups=groups)
    return parts.reshape((4 * values.shape[0],) + values.shape[1:])


def swap_cores(values):
    return lax.ppermute(values, "rep", [(0, 1), (1, 0), (2, 3), (3, 2)])


def send(values, distance, cross=False):
    pairs = []
    for z in range(16):
        for rep in range(4):
            target = (z + (-distance if rep % 2 else distance)) % 16
            pairs.append((z * 4 + rep, target * 4 + (rep ^ 1 if cross else rep)))
    return lax.ppermute(values, ring, pairs)


def matmul_nt(a, b):
    return lax.dot_general(a, b, (((1,), (1,)), ((), ())), preferred_element_type=jnp.float32)


def matmul_tn(a, b):
    return lax.dot_general(a, b, (((0,), (0,)), ((), ())), preferred_element_type=jnp.float32)


def call(kernel, outs, args, flops=0, scratch=()):
    vmem = pl.BlockSpec(memory_space=pltpu.VMEM)
    moved = sum(v.size * v.dtype.itemsize for v in tuple(args) + tuple(outs))
    return pl.pallas_call(
        kernel,
        out_shape=outs,
        in_specs=[vmem] * len(args),
        out_specs=tuple(vmem for _ in outs),
        scratch_shapes=scratch,
        compiler_params=pltpu.CompilerParams(vmem_limit_bytes=40 * 1024 * 1024),
        cost_estimate=pl.CostEstimate(flops=flops, bytes_accessed=moved, transcendentals=0),
    )(*args)


def partial_kernel(groups, dots, grad_ref, own_ref, other_ref, *refs):
    outs = refs[-len(groups) :]
    add_ref = refs[0] if len(refs) > len(groups) else None
    core = lax.rem(lax.axis_index("rep"), 2)
    z = lax.axis_index("col")
    width = own_ref.shape[0]
    blocks = [
        (out_ref, i, flipped, lax.rem(z + (1 - 2 * core) * step + 16, 16))
        for (steps, flipped), out_ref in zip(groups, outs)
        for i, step in enumerate(steps)
    ]
    start = 0
    for count in dots:
        taken_now = blocks[start : start + count]
        rows = jnp.concatenate([grad_ref[place(chip, core)] for _, _, _, chip in taken_now], axis=0)
        for side, ref in enumerate((own_ref, other_ref)):
            part = matmul_nt(rows, ref[...]).reshape(count, -1, width)
            for j, (out_ref, i, flipped, _) in enumerate(taken_now):
                at = (1 - side if flipped else side) * width
                value = part[j]
                if add_ref is not None and start + j == 0:
                    value = value + add_ref[0, :, at : at + width].astype(jnp.float32)
                out_ref[i, :, at : at + width] = value.astype(out_ref.dtype)
        start += count


def partials(groups, dots, grad_blocks, weights, *add):
    rows, depth = grad_blocks.shape[1:]
    width = weights[0].shape[0]
    return call(
        functools.partial(partial_kernel, groups, dots),
        [jax.ShapeDtypeStruct((len(g[0]), rows, 2 * width), jnp.bfloat16) for g in groups],
        (grad_blocks, *weights, *add),
        flops=12 * sum(dots) * rows * depth * width,
    )


def first_kernel(own_ref, cross_ref, rest_ref, other_ref, send_ref, middle_ref, here_ref):
    def total(i, *refs):
        return sum(ref[i].astype(jnp.float32) for ref in refs)

    dtype = send_ref.dtype
    send_ref[0, 0] = total(0, own_ref, rest_ref).astype(dtype)
    send_ref[0, 1] = total(0, cross_ref, other_ref).astype(dtype)
    send_ref[1, 0] = total(2, own_ref, rest_ref).astype(dtype)
    send_ref[1, 1] = total(2, cross_ref, other_ref).astype(dtype)
    middle_ref[0] = total(1, own_ref, rest_ref)
    middle_ref[1] = total(1, cross_ref, other_ref)
    here_ref[0] = total(3, own_ref, rest_ref)
    here_ref[1] = total(3, cross_ref)


def second_kernel(moved_ref, middle_ref, here_ref, own_ref, cross_ref, stay_ref, swap_ref):
    width = own_ref.shape[2]
    ahead = (middle_ref[...] + moved_ref[0].astype(jnp.float32)).astype(own_ref.dtype)
    own_ref[...] = ahead[:, :, :width]
    cross_ref[...] = ahead[:, :, width:]
    here = here_ref[...] + moved_ref[1].astype(jnp.float32)
    stay_ref[...] = here[:, :, :width]
    swap_ref[...] = here[:, :, width:].astype(swap_ref.dtype)


def third_kernel(own_ref, cross_ref, stay_ref, swap_ref, out_ref):
    half = own_ref.shape[1]
    core = lax.rem(lax.axis_index("rep"), 2)
    for i, place_of in enumerate((core, 1 - core)):
        other = cross_ref[1 - i].astype(jnp.float32) + swap_ref[1 - i].astype(jnp.float32)
        part = stay_ref[i] + own_ref[i].astype(jnp.float32) + other
        rows = pl.ds(pl.multiple_of(place_of * half, half), half)
        out_ref[rows, :] = part.astype(out_ref.dtype)


def taken(step, *args):
    return lax.cond(
        lax.axis_index("col") < 16,
        step,
        lambda *a: jax.tree.map(lambda v: jnp.zeros(v.shape, v.dtype), jax.eval_shape(step, *a)),
        *args,
    )


def gather_and_round(gelu_grad, weight):
    line = gather(gelu_grad, along_x[0] + along_y[1])
    weight_other = swap_cores(weight)
    grad_tokens = gather(line, along_y[0] + along_x[1])
    grad_blocks = grad_tokens.reshape((16,) + gelu_grad.shape)

    weights = weight, weight_other
    far, ahead = partials(first_groups, (5,), grad_blocks, weights)
    far, next_blocks = lax.optimization_barrier((far, grad_blocks))
    far, own = send(far, 2), send(ahead, 1)
    behind = partials(early_groups, (4,), next_blocks, weights)[0]
    behind, later_blocks = lax.optimization_barrier((behind, next_blocks))
    cross = send(behind, -1, cross=True)
    rest, for_sibling = partials(late_groups, (7,), later_blocks, weights, far)
    rest, last_blocks = lax.optimization_barrier((rest, later_blocks))
    kept = jnp.where(lax.axis_index("col") < 16, last_blocks, jnp.zeros_like(last_blocks))
    rest_other = swap_cores(for_sibling)

    both = (2,) + rest.shape[1:]
    outs = [
        jax.ShapeDtypeStruct((2,) + both, jnp.bfloat16),
        jax.ShapeDtypeStruct(both, jnp.float32),
        jax.ShapeDtypeStruct(both, jnp.float32),
    ]
    return (*call(first_kernel, outs, (own, cross, rest, rest_other)), kept)


def weight_kernel(sibling, input_ref, grad_ref, *refs):
    first_ref = refs[0] if len(refs) == 3 else None
    out_ref, rows_ref = refs[-2:]
    half, depth = grad_ref.shape[1:]
    core = lax.rem(lax.axis_index("rep"), 2)
    core = 1 - core if sibling else core
    for chip in range(16):
        at = jnp.where(core == 0, (chip % 4) * 4 + chip // 4, chip)
        rows = pl.ds(pl.multiple_of(at * half, half), half)
        rows_ref[rows, :] = input_ref[chip, core]
    tile = 256
    for start in range(0, depth, tile):
        grad = grad_ref[:, :, start : start + tile].reshape(16 * half, tile)
        part = matmul_tn(rows_ref[...], grad)
        if first_ref is not None:
            part = part + first_ref[:, start : start + tile]
        out_ref[:, start : start + tile] = part


def weight_gradient(sibling, input_whole, grad_blocks, *first):
    tokens, width = input_whole.shape
    half, depth = grad_blocks.shape[1:]
    out = jax.ShapeDtypeStruct((width, depth), jnp.float32)
    return call(
        functools.partial(weight_kernel, sibling),
        [out],
        (input_whole.reshape(16, 2, half, width), grad_blocks, *first),
        flops=(1 if sibling else 40) * tokens * width * depth,
        scratch=[pltpu.VMEM((tokens // 2, width), jnp.bfloat16)],
    )[0]


def local(layer_input, weight, gelu_input, upstream):
    tokens, width = layer_input.shape
    half = tokens // 2
    f32, bf16 = jnp.float32, jnp.bfloat16

    input_whole = lax.all_gather(layer_input, "col", axis=0, tiled=True)
    gelu_grad = (upstream.astype(f32) * gelu_slope(gelu_input.astype(f32))).astype(bf16)

    to_send, middle, here, grad_blocks = taken(gather_and_round, gelu_grad, weight)

    moved = send(to_send, 2)
    grad_other = swap_cores(grad_blocks)
    grad_weight = weight_gradient(False, input_whole, grad_blocks)
    grad_weight = weight_gradient(True, input_whole, grad_other, grad_weight)
    moved, grad_weight = lax.optimization_barrier((moved, grad_weight))
    part = (2, half, width)
    outs = [jax.ShapeDtypeStruct(part, t) for t in (bf16, bf16, f32, bf16)]
    own, cross, stay, swapped = call(second_kernel, outs, (moved, middle, here))
    last = send(own, 4), send(cross, 4, cross=True), stay, swap_cores(swapped)
    outs = [jax.ShapeDtypeStruct((tokens, width), bf16)]
    grad_input = call(third_kernel, outs, last)[0]
    return (grad_input, grad_weight)


def solution(mesh):
    in_specs = (
        P("col", ("row", "rep")),
        P(("row", "rep"), "col"),
        P(("row", "rep"), "col"),
        P(("row", "rep"), "col"),
    )
    out_specs = (P("col", ("row", "rep")), P(("row", "rep"), "col"))
    return jax.shard_map(local, mesh=mesh, in_specs=in_specs, out_specs=out_specs, check_vma=False)
```

```python
import functools
import math

import jax
import jax.numpy as jnp
from jax import lax
from jax.experimental import pallas as pl
from jax.experimental.pallas import tpu as pltpu
from jax.sharding import PartitionSpec as P

cubic_term = 0.044715
plane = ("row", "rep")
ring = ("col", "rep")


def gelu_slope(values):
    scale = math.sqrt(2.0 / math.pi)
    inner = scale * (values + cubic_term * values * values * values)
    tangent = jnp.tanh(inner)
    return 0.5 * (1.0 + tangent) + 0.5 * values * (1.0 - tangent * tangent) * scale * (
        1.0 + 3.0 * cubic_term * values * values
    )


def index(x, y, core):
    return ((x * 2 + y % 2) * 2 + y // 2) * 2 + core


y_order = (0, 2, 1, 3)
along_x = [[[index(x, y, core) for x in range(4)] for y in y_order] for core in range(2)]
along_y = [[[index(x, y, core) for y in y_order] for x in range(4)] for core in range(2)]


first_groups = (((8,), False), ((7, 5, 3, 1), False))
early_groups = (((-7, -5, -3, -1), True),)
late_groups = (((6, 4, 2, 0), False), ((-6, -4, -2), True))


def place(chip, core):
    turned = lax.rem(chip, 4) * 4 + lax.div(chip, 4)
    return jnp.where(core == 0, turned, chip)


def gather(values, groups):
    copies = jnp.broadcast_to(values[None], (4,) + values.shape)
    parts = lax.all_to_all(copies, plane, 0, 0, axis_index_groups=groups)
    return parts.reshape((4 * values.shape[0],) + values.shape[1:])


def swap_cores(values):
    return lax.ppermute(values, "rep", [(0, 1), (1, 0), (2, 3), (3, 2)])


def send(values, distance, cross=False):
    pairs = []
    for z in range(16):
        for rep in range(4):
            target = (z + (-distance if rep % 2 else distance)) % 16
            pairs.append((z * 4 + rep, target * 4 + (rep ^ 1 if cross else rep)))
    return lax.ppermute(values, ring, pairs)


def matmul_nt(a, b):
    return lax.dot_general(a, b, (((1,), (1,)), ((), ())), preferred_element_type=jnp.float32)


def matmul_tn(a, b):
    return lax.dot_general(a, b, (((0,), (0,)), ((), ())), preferred_element_type=jnp.float32)


def call(kernel, outs, args, flops=0, scratch=()):
    vmem = pl.BlockSpec(memory_space=pltpu.VMEM)
    moved = sum(v.size * v.dtype.itemsize for v in tuple(args) + tuple(outs))
    return pl.pallas_call(
        kernel,
        out_shape=outs,
        in_specs=[vmem] * len(args),
        out_specs=tuple(vmem for _ in outs),
        scratch_shapes=scratch,
        compiler_params=pltpu.CompilerParams(vmem_limit_bytes=40 * 1024 * 1024),
        cost_estimate=pl.CostEstimate(flops=flops, bytes_accessed=moved, transcendentals=0),
    )(*args)


def partial_kernel(groups, dots, grad_ref, own_ref, other_ref, *refs):
    outs = refs[-len(groups) :]
    add_ref = refs[0] if len(refs) > len(groups) else None
    core = lax.rem(lax.axis_index("rep"), 2)
    z = lax.axis_index("col")
    width = own_ref.shape[0]
    blocks = [
        (out_ref, i, flipped, lax.rem(z + (1 - 2 * core) * step + 16, 16))
        for (steps, flipped), out_ref in zip(groups, outs)
        for i, step in enumerate(steps)
    ]
    start = 0
    for count in dots:
        taken_now = blocks[start : start + count]
        rows = jnp.concatenate([grad_ref[place(chip, core)] for _, _, _, chip in taken_now], axis=0)
        for side, ref in enumerate((own_ref, other_ref)):
            part = matmul_nt(rows, ref[...]).reshape(count, -1, width)
            for j, (out_ref, i, flipped, _) in enumerate(taken_now):
                at = (1 - side if flipped else side) * width
                value = part[j]
                if add_ref is not None and start + j == 0:
                    value = value + add_ref[0, :, at : at + width].astype(jnp.float32)
                out_ref[i, :, at : at + width] = value.astype(out_ref.dtype)
        start += count


def partials(groups, dots, grad_blocks, weights, *add):
    rows, depth = grad_blocks.shape[1:]
    width = weights[0].shape[0]
    return call(
        functools.partial(partial_kernel, groups, dots),
        [jax.ShapeDtypeStruct((len(g[0]), rows, 2 * width), jnp.bfloat16) for g in groups],
        (grad_blocks, *weights, *add),
        flops=12 * sum(dots) * rows * depth * width,
    )


def first_kernel(own_ref, cross_ref, rest_ref, other_ref, send_ref, middle_ref, here_ref):
    def total(i, *refs):
        return sum(ref[i].astype(jnp.float32) for ref in refs)

    dtype = send_ref.dtype
    send_ref[0, 0] = total(0, own_ref, rest_ref).astype(dtype)
    send_ref[0, 1] = total(0, cross_ref, other_ref).astype(dtype)
    send_ref[1, 0] = total(2, own_ref, rest_ref).astype(dtype)
    send_ref[1, 1] = total(2, cross_ref, other_ref).astype(dtype)
    middle_ref[0] = total(1, own_ref, rest_ref)
    middle_ref[1] = total(1, cross_ref, other_ref)
    here_ref[0] = total(3, own_ref, rest_ref)
    here_ref[1] = total(3, cross_ref)


def second_kernel(moved_ref, middle_ref, here_ref, own_ref, cross_ref, stay_ref, swap_ref):
    width = own_ref.shape[2]
    ahead = (middle_ref[...] + moved_ref[0].astype(jnp.float32)).astype(own_ref.dtype)
    own_ref[...] = ahead[:, :, :width]
    cross_ref[...] = ahead[:, :, width:]
    here = here_ref[...] + moved_ref[1].astype(jnp.float32)
    stay_ref[...] = here[:, :, :width]
    swap_ref[...] = here[:, :, width:].astype(swap_ref.dtype)


def third_kernel(own_ref, cross_ref, stay_ref, swap_ref, out_ref):
    half = own_ref.shape[1]
    core = lax.rem(lax.axis_index("rep"), 2)
    for i, place_of in enumerate((core, 1 - core)):
        other = cross_ref[1 - i].astype(jnp.float32) + swap_ref[1 - i].astype(jnp.float32)
        part = stay_ref[i] + own_ref[i].astype(jnp.float32) + other
        rows = pl.ds(pl.multiple_of(place_of * half, half), half)
        out_ref[rows, :] = part.astype(out_ref.dtype)


def taken(step, *args):
    return lax.cond(
        lax.axis_index("col") < 16,
        step,
        lambda *a: jax.tree.map(lambda v: jnp.zeros(v.shape, v.dtype), jax.eval_shape(step, *a)),
        *args,
    )


def first_gather(gelu_grad, block):
    return gather(gelu_grad, along_x[0] + along_y[1]), send(block, -4)


def gather_and_round(line, weight, block, input_4):
    weight_other = swap_cores(weight)
    grad_tokens = gather(line, along_y[0] + along_x[1])
    input_8 = send(input_4[0], -4)
    input_2_6 = send(jnp.stack([block, input_4]), -2)
    grad_tokens, input_2_6 = lax.optimization_barrier((grad_tokens, input_2_6))
    evens = jnp.stack([block, input_2_6[0], input_4, input_2_6[1]])
    odds = send(evens, -1)
    grad_blocks = grad_tokens.reshape((16,) + (line.shape[0] // 4, line.shape[1]))

    weights = weight, weight_other
    far, ahead = partials(first_groups, (5,), grad_blocks, weights)
    far, next_blocks = lax.optimization_barrier((far, grad_blocks))
    far, own = send(far, 2), send(ahead, 1)
    behind = partials(early_groups, (4,), next_blocks, weights)[0]
    behind, later_blocks = lax.optimization_barrier((behind, next_blocks))
    cross = send(behind, -1, cross=True)
    rest, for_sibling = partials(late_groups, (7,), later_blocks, weights, far)
    rest, last_blocks = lax.optimization_barrier((rest, later_blocks))
    kept = jnp.where(lax.axis_index("col") < 16, last_blocks, jnp.zeros_like(last_blocks))
    rest_other = swap_cores(for_sibling)

    width = weight.shape[0]
    half = block.shape[1]
    parts = [v[..., width:].reshape(-1, half, width) for v in (evens[1:], odds, input_8)]
    gathered = evens, odds, input_8, jnp.concatenate(parts)

    both = (2,) + rest.shape[1:]
    outs = [
        jax.ShapeDtypeStruct((2,) + both, jnp.bfloat16),
        jax.ShapeDtypeStruct(both, jnp.float32),
        jax.ShapeDtypeStruct(both, jnp.float32),
    ]
    return (*call(first_kernel, outs, (own, cross, rest, rest_other)), kept, *gathered)


def weight_kernel(sibling, evens_ref, odds_ref, far_ref, other_ref, grad_ref, *refs):
    first_ref = refs[0] if len(refs) == 3 else None
    out_ref, rows_ref = refs[-2:]
    half, depth = grad_ref.shape[1:]
    width = out_ref.shape[0]
    core = lax.rem(lax.axis_index("rep"), 2)
    z = lax.axis_index("col")
    holder = 1 - core if sibling else core
    whose = 1 if sibling else 0
    blocks = [(2 * i, evens_ref[i, whose, :, :width]) for i in range(4)]
    blocks += [(2 * i + 1, odds_ref[i, whose, :, :width]) for i in range(4)]
    blocks += [(8, other_ref[14] if sibling else far_ref[:, :width])]
    blocks += [
        (-step, other_ref[2 * i + 1 - whose]) for i, step in enumerate((2, 4, 6, 1, 3, 5, 7))
    ]
    for step, block in blocks:
        chip = lax.rem(z + (1 - 2 * core) * step + 16, 16)
        rows = pl.ds(pl.multiple_of(place(chip, holder) * half, half), half)
        rows_ref[rows, :] = block
    tile = 256
    for start in range(0, depth, tile):
        grad = grad_ref[:, :, start : start + tile].reshape(16 * half, tile)
        part = matmul_tn(rows_ref[...], grad)
        if first_ref is not None:
            part = part + first_ref[:, start : start + tile]
        out_ref[:, start : start + tile] = part


def weight_gradient(sibling, gathered, grad_blocks, *first):
    half, depth = grad_blocks.shape[1:]
    width = gathered[3].shape[2]
    out = jax.ShapeDtypeStruct((width, depth), jnp.float32)
    return call(
        functools.partial(weight_kernel, sibling),
        [out],
        (*gathered, grad_blocks, *first),
        flops=(1 if sibling else 40) * 32 * half * width * depth,
        scratch=[pltpu.VMEM((16 * half, width), jnp.bfloat16)],
    )[0]


def local(layer_input, weight, gelu_input, upstream):
    tokens, width = layer_input.shape
    half = tokens // 2
    f32, bf16 = jnp.float32, jnp.bfloat16

    block = jnp.concatenate(
        [v.reshape(2, half, width) for v in (layer_input, swap_cores(layer_input))], axis=2
    )
    block = jnp.where(lax.axis_index("rep") % 2 == 0, block, block[::-1])
    gelu_grad = (upstream.astype(f32) * gelu_slope(gelu_input.astype(f32))).astype(bf16)
    gelu_grad, block = lax.optimization_barrier((gelu_grad, block))

    line, input_4 = taken(first_gather, gelu_grad, block)
    to_send, middle, here, grad_blocks, *gathered, for_sibling = taken(
        gather_and_round, line, weight, block, input_4
    )

    moved = send(to_send, 2)
    grad_other = swap_cores(grad_blocks)
    gathered = (*gathered, swap_cores(for_sibling))
    grad_weight = weight_gradient(False, gathered, grad_blocks)
    grad_weight = weight_gradient(True, gathered, grad_other, grad_weight)
    moved, grad_weight = lax.optimization_barrier((moved, grad_weight))
    part = (2, half, width)
    outs = [jax.ShapeDtypeStruct(part, t) for t in (bf16, bf16, f32, bf16)]
    own, cross, stay, swapped = call(second_kernel, outs, (moved, middle, here))
    last = send(own, 4), send(cross, 4, cross=True), stay, swap_cores(swapped)
    outs = [jax.ShapeDtypeStruct((tokens, width), bf16)]
    grad_input = call(third_kernel, outs, last)[0]
    return (grad_input, grad_weight)


def solution(mesh):
    in_specs = (
        P("col", ("row", "rep")),
        P(("row", "rep"), "col"),
        P(("row", "rep"), "col"),
        P(("row", "rep"), "col"),
    )
    out_specs = (P("col", ("row", "rep")), P(("row", "rep"), "col"))
    return jax.shard_map(local, mesh=mesh, in_specs=in_specs, out_specs=out_specs, check_vma=False)
```

```python
import functools
import math

import jax
import jax.numpy as jnp
from jax import lax
from jax.experimental import pallas as pl
from jax.experimental.pallas import tpu as pltpu
from jax.sharding import PartitionSpec as P

cubic_term = 0.044715
plane = ("row", "rep")
ring = ("col", "rep")


def gelu_slope(values):
    scale = math.sqrt(2.0 / math.pi)
    inner = scale * (values + cubic_term * values * values * values)
    tangent = jnp.tanh(inner)
    return 0.5 * (1.0 + tangent) + 0.5 * values * (1.0 - tangent * tangent) * scale * (
        1.0 + 3.0 * cubic_term * values * values
    )


def index(x, y, core):
    return ((x * 2 + y % 2) * 2 + y // 2) * 2 + core


y_order = (0, 2, 1, 3)
along_x = [[[index(x, y, core) for x in range(4)] for y in y_order] for core in range(2)]
along_y = [[[index(x, y, core) for y in y_order] for x in range(4)] for core in range(2)]


early_groups = (((8,), False), ((7, 5, 3, 1), False), ((-7, -5, -3, -1), True))
late_groups = (((6, 4, 2, 0), False), ((-6, -4, -2), True))


def place(chip, core):
    turned = lax.rem(chip, 4) * 4 + lax.div(chip, 4)
    return jnp.where(core == 0, turned, chip)


def gather(values, groups):
    copies = jnp.broadcast_to(values[None], (4,) + values.shape)
    parts = lax.all_to_all(copies, plane, 0, 0, axis_index_groups=groups)
    return parts.reshape((4 * values.shape[0],) + values.shape[1:])


def swap_cores(values):
    return lax.ppermute(values, "rep", [(0, 1), (1, 0), (2, 3), (3, 2)])


def send(values, distance, cross=False):
    pairs = []
    for z in range(16):
        for rep in range(4):
            target = (z + (-distance if rep % 2 else distance)) % 16
            pairs.append((z * 4 + rep, target * 4 + (rep ^ 1 if cross else rep)))
    return lax.ppermute(values, ring, pairs)


def matmul_nt(a, b):
    return lax.dot_general(a, b, (((1,), (1,)), ((), ())), preferred_element_type=jnp.float32)


def matmul_tn(a, b):
    return lax.dot_general(a, b, (((0,), (0,)), ((), ())), preferred_element_type=jnp.float32)


def call(kernel, outs, args, flops=0, scratch=()):
    vmem = pl.BlockSpec(memory_space=pltpu.VMEM)
    moved = sum(v.size * v.dtype.itemsize for v in tuple(args) + tuple(outs))
    return pl.pallas_call(
        kernel,
        out_shape=outs,
        in_specs=[vmem] * len(args),
        out_specs=tuple(vmem for _ in outs),
        scratch_shapes=scratch,
        compiler_params=pltpu.CompilerParams(vmem_limit_bytes=40 * 1024 * 1024),
        cost_estimate=pl.CostEstimate(flops=flops, bytes_accessed=moved, transcendentals=0),
    )(*args)


def partial_kernel(groups, dots, grad_ref, own_ref, other_ref, *refs):
    outs = refs[-len(groups) :]
    add_ref = refs[0] if len(refs) > len(groups) else None
    core = lax.rem(lax.axis_index("rep"), 2)
    z = lax.axis_index("col")
    width = own_ref.shape[0]
    blocks = [
        (out_ref, i, flipped, lax.rem(z + (1 - 2 * core) * step + 16, 16))
        for (steps, flipped), out_ref in zip(groups, outs)
        for i, step in enumerate(steps)
    ]
    start = 0
    for count in dots:
        taken_now = blocks[start : start + count]
        rows = jnp.concatenate([grad_ref[place(chip, core)] for _, _, _, chip in taken_now], axis=0)
        for side, ref in enumerate((own_ref, other_ref)):
            part = matmul_nt(rows, ref[...]).reshape(count, -1, width)
            for j, (out_ref, i, flipped, _) in enumerate(taken_now):
                at = (1 - side if flipped else side) * width
                value = part[j]
                if add_ref is not None and start + j == 0:
                    value = value + add_ref[0, :, at : at + width].astype(jnp.float32)
                out_ref[i, :, at : at + width] = value.astype(out_ref.dtype)
        start += count


def partials(groups, dots, grad_blocks, weights, *add):
    rows, depth = grad_blocks.shape[1:]
    width = weights[0].shape[0]
    return call(
        functools.partial(partial_kernel, groups, dots),
        [jax.ShapeDtypeStruct((len(g[0]), rows, 2 * width), jnp.bfloat16) for g in groups],
        (grad_blocks, *weights, *add),
        flops=12 * sum(dots) * rows * depth * width,
    )


def first_kernel(own_ref, cross_ref, rest_ref, other_ref, send_ref, middle_ref, here_ref):
    def total(i, *refs):
        return sum(ref[i].astype(jnp.float32) for ref in refs)

    dtype = send_ref.dtype
    send_ref[0, 0] = total(0, own_ref, rest_ref).astype(dtype)
    send_ref[0, 1] = total(0, cross_ref, other_ref).astype(dtype)
    send_ref[1, 0] = total(2, own_ref, rest_ref).astype(dtype)
    send_ref[1, 1] = total(2, cross_ref, other_ref).astype(dtype)
    middle_ref[0] = total(1, own_ref, rest_ref)
    middle_ref[1] = total(1, cross_ref, other_ref)
    here_ref[0] = total(3, own_ref, rest_ref)
    here_ref[1] = total(3, cross_ref)


def second_kernel(moved_ref, middle_ref, here_ref, own_ref, cross_ref, stay_ref, swap_ref):
    width = own_ref.shape[2]
    ahead = (middle_ref[...] + moved_ref[0].astype(jnp.float32)).astype(own_ref.dtype)
    own_ref[...] = ahead[:, :, :width]
    cross_ref[...] = ahead[:, :, width:]
    here = here_ref[...] + moved_ref[1].astype(jnp.float32)
    stay_ref[...] = here[:, :, :width]
    swap_ref[...] = here[:, :, width:].astype(swap_ref.dtype)


def third_kernel(own_ref, cross_ref, stay_ref, swap_ref, out_ref):
    half = own_ref.shape[1]
    core = lax.rem(lax.axis_index("rep"), 2)
    for i, place_of in enumerate((core, 1 - core)):
        other = cross_ref[1 - i].astype(jnp.float32) + swap_ref[1 - i].astype(jnp.float32)
        part = stay_ref[i] + own_ref[i].astype(jnp.float32) + other
        rows = pl.ds(pl.multiple_of(place_of * half, half), half)
        out_ref[rows, :] = part.astype(out_ref.dtype)


def taken(step, *args):
    return lax.cond(
        lax.axis_index("col") < 16,
        step,
        lambda *a: jax.tree.map(lambda v: jnp.zeros(v.shape, v.dtype), jax.eval_shape(step, *a)),
        *args,
    )


def gather_and_round(gelu_grad, weight):
    line = gather(gelu_grad, along_x[0] + along_y[1])
    weight_other = swap_cores(weight)
    grad_tokens = gather(line, along_y[0] + along_x[1])
    grad_blocks = grad_tokens.reshape((16,) + gelu_grad.shape)

    weights = weight, weight_other
    far, ahead, behind = partials(early_groups, (5, 4), grad_blocks, weights)
    far, later_blocks = lax.optimization_barrier((far, grad_blocks))
    far = send(far, 2)
    own, cross = send(ahead, 1), send(behind, -1, cross=True)
    rest, for_sibling = partials(late_groups, (7,), later_blocks, weights, far)
    rest_other = swap_cores(for_sibling)

    both = (2,) + rest.shape[1:]
    outs = [
        jax.ShapeDtypeStruct((2,) + both, jnp.bfloat16),
        jax.ShapeDtypeStruct(both, jnp.float32),
        jax.ShapeDtypeStruct(both, jnp.float32),
    ]
    return (*call(first_kernel, outs, (own, cross, rest, rest_other)), grad_blocks)


def weight_kernel(sibling, input_ref, grad_ref, *refs):
    first_ref = refs[0] if len(refs) == 3 else None
    out_ref, rows_ref = refs[-2:]
    half, depth = grad_ref.shape[1:]
    core = lax.rem(lax.axis_index("rep"), 2)
    core = 1 - core if sibling else core
    for chip in range(16):
        at = jnp.where(core == 0, (chip % 4) * 4 + chip // 4, chip)
        rows = pl.ds(pl.multiple_of(at * half, half), half)
        rows_ref[rows, :] = input_ref[chip, core]
    tile = 256
    for start in range(0, depth, tile):
        grad = grad_ref[:, :, start : start + tile].reshape(16 * half, tile)
        part = matmul_tn(rows_ref[...], grad)
        if first_ref is not None:
            part = part + first_ref[:, start : start + tile]
        out_ref[:, start : start + tile] = part


def weight_gradient(sibling, input_whole, grad_blocks, *first):
    tokens, width = input_whole.shape
    half, depth = grad_blocks.shape[1:]
    out = jax.ShapeDtypeStruct((width, depth), jnp.float32)
    return call(
        functools.partial(weight_kernel, sibling),
        [out],
        (input_whole.reshape(16, 2, half, width), grad_blocks, *first),
        flops=(1 if sibling else 40) * tokens * width * depth,
        scratch=[pltpu.VMEM((tokens // 2, width), jnp.bfloat16)],
    )[0]


def local(layer_input, weight, gelu_input, upstream):
    tokens, width = layer_input.shape
    half = tokens // 2
    f32, bf16 = jnp.float32, jnp.bfloat16

    input_whole = lax.all_gather(layer_input, "col", axis=0, tiled=True)
    gelu_grad = (upstream.astype(f32) * gelu_slope(gelu_input.astype(f32))).astype(bf16)

    to_send, middle, here, grad_blocks = taken(gather_and_round, gelu_grad, weight)

    moved = send(to_send, 2)
    grad_other = swap_cores(grad_blocks)
    grad_weight = weight_gradient(False, input_whole, grad_blocks)
    grad_weight = weight_gradient(True, input_whole, grad_other, grad_weight)
    moved, grad_weight = lax.optimization_barrier((moved, grad_weight))
    part = (2, half, width)
    outs = [jax.ShapeDtypeStruct(part, t) for t in (bf16, bf16, f32, bf16)]
    own, cross, stay, swapped = call(second_kernel, outs, (moved, middle, here))
    last = send(own, 4), send(cross, 4, cross=True), stay, swap_cores(swapped)
    outs = [jax.ShapeDtypeStruct((tokens, width), bf16)]
    grad_input = call(third_kernel, outs, last)[0]
    return (grad_input, grad_weight)


def solution(mesh):
    in_specs = (
        P("col", ("row", "rep")),
        P(("row", "rep"), "col"),
        P(("row", "rep"), "col"),
        P(("row", "rep"), "col"),
    )
    out_specs = (P("col", ("row", "rep")), P(("row", "rep"), "col"))
    return jax.shard_map(local, mesh=mesh, in_specs=in_specs, out_specs=out_specs, check_vma=False)
```

```python
import functools
import math

import jax
import jax.numpy as jnp
from jax import lax
from jax.experimental import pallas as pl
from jax.experimental.pallas import tpu as pltpu
from jax.sharding import PartitionSpec as P

cubic_term = 0.044715
plane = ("row", "rep")
ring = ("col", "rep")


def gelu_slope(values):
    scale = math.sqrt(2.0 / math.pi)
    inner = scale * (values + cubic_term * values * values * values)
    tangent = jnp.tanh(inner)
    return 0.5 * (1.0 + tangent) + 0.5 * values * (1.0 - tangent * tangent) * scale * (
        1.0 + 3.0 * cubic_term * values * values
    )


def index(x, y, core):
    return ((x * 2 + y % 2) * 2 + y // 2) * 2 + core


y_order = (0, 2, 1, 3)
along_x = [[[index(x, y, core) for x in range(4)] for y in y_order] for core in range(2)]
along_y = [[[index(x, y, core) for y in y_order] for x in range(4)] for core in range(2)]


early_groups = (((8,), False), ((7, 5, 3, 1), False), ((-7, -5, -3, -1), True))
late_groups = (((6, 4, 2, 0), False), ((-6, -4, -2), True))


def place(chip, core):
    turned = lax.rem(chip, 4) * 4 + lax.div(chip, 4)
    return jnp.where(core == 0, turned, chip)


def gather(values, groups):
    copies = jnp.broadcast_to(values[None], (4,) + values.shape)
    parts = lax.all_to_all(copies, plane, 0, 0, axis_index_groups=groups)
    return parts.reshape((4 * values.shape[0],) + values.shape[1:])


def swap_cores(values):
    return lax.ppermute(values, "rep", [(0, 1), (1, 0), (2, 3), (3, 2)])


def send(values, distance, cross=False):
    pairs = []
    for z in range(16):
        for rep in range(4):
            target = (z + (-distance if rep % 2 else distance)) % 16
            pairs.append((z * 4 + rep, target * 4 + (rep ^ 1 if cross else rep)))
    return lax.ppermute(values, ring, pairs)


def matmul_nt(a, b):
    return lax.dot_general(a, b, (((1,), (1,)), ((), ())), preferred_element_type=jnp.float32)


def matmul_tn(a, b):
    return lax.dot_general(a, b, (((0,), (0,)), ((), ())), preferred_element_type=jnp.float32)


def call(kernel, outs, args, flops=0, scratch=()):
    vmem = pl.BlockSpec(memory_space=pltpu.VMEM)
    moved = sum(v.size * v.dtype.itemsize for v in tuple(args) + tuple(outs))
    return pl.pallas_call(
        kernel,
        out_shape=outs,
        in_specs=[vmem] * len(args),
        out_specs=tuple(vmem for _ in outs),
        scratch_shapes=scratch,
        compiler_params=pltpu.CompilerParams(vmem_limit_bytes=40 * 1024 * 1024),
        cost_estimate=pl.CostEstimate(flops=flops, bytes_accessed=moved, transcendentals=0),
    )(*args)


def partial_kernel(groups, dots, grad_ref, own_ref, other_ref, *refs):
    outs = refs[-len(groups) :]
    add_ref = refs[0] if len(refs) > len(groups) else None
    core = lax.rem(lax.axis_index("rep"), 2)
    z = lax.axis_index("col")
    width = own_ref.shape[0]
    blocks = [
        (out_ref, i, flipped, lax.rem(z + (1 - 2 * core) * step + 16, 16))
        for (steps, flipped), out_ref in zip(groups, outs)
        for i, step in enumerate(steps)
    ]
    start = 0
    for count in dots:
        taken_now = blocks[start : start + count]
        rows = jnp.concatenate([grad_ref[place(chip, core)] for _, _, _, chip in taken_now], axis=0)
        for side, ref in enumerate((own_ref, other_ref)):
            part = matmul_nt(rows, ref[...]).reshape(count, -1, width)
            for j, (out_ref, i, flipped, _) in enumerate(taken_now):
                at = (1 - side if flipped else side) * width
                value = part[j]
                if add_ref is not None and start + j == 0:
                    value = value + add_ref[0, :, at : at + width].astype(jnp.float32)
                out_ref[i, :, at : at + width] = value.astype(out_ref.dtype)
        start += count


def partials(groups, dots, grad_blocks, weights, *add):
    rows, depth = grad_blocks.shape[1:]
    width = weights[0].shape[0]
    return call(
        functools.partial(partial_kernel, groups, dots),
        [jax.ShapeDtypeStruct((len(g[0]), rows, 2 * width), jnp.bfloat16) for g in groups],
        (grad_blocks, *weights, *add),
        flops=12 * sum(dots) * rows * depth * width,
    )


def first_kernel(own_ref, cross_ref, rest_ref, other_ref, send_ref, middle_ref, here_ref):
    def total(i, *refs):
        return sum(ref[i].astype(jnp.float32) for ref in refs)

    dtype = send_ref.dtype
    send_ref[0, 0] = total(0, own_ref, rest_ref).astype(dtype)
    send_ref[0, 1] = total(0, cross_ref, other_ref).astype(dtype)
    send_ref[1, 0] = total(2, own_ref, rest_ref).astype(dtype)
    send_ref[1, 1] = total(2, cross_ref, other_ref).astype(dtype)
    middle_ref[0] = total(1, own_ref, rest_ref)
    middle_ref[1] = total(1, cross_ref, other_ref)
    here_ref[0] = total(3, own_ref, rest_ref)
    here_ref[1] = total(3, cross_ref)


def second_kernel(moved_ref, middle_ref, here_ref, own_ref, cross_ref, stay_ref, swap_ref):
    width = own_ref.shape[2]
    ahead = (middle_ref[...] + moved_ref[0].astype(jnp.float32)).astype(own_ref.dtype)
    own_ref[...] = ahead[:, :, :width]
    cross_ref[...] = ahead[:, :, width:]
    here = here_ref[...] + moved_ref[1].astype(jnp.float32)
    stay_ref[...] = here[:, :, :width]
    swap_ref[...] = here[:, :, width:].astype(swap_ref.dtype)


def third_kernel(own_ref, cross_ref, stay_ref, swap_ref, out_ref):
    half = own_ref.shape[1]
    core = lax.rem(lax.axis_index("rep"), 2)
    for i, place_of in enumerate((core, 1 - core)):
        other = cross_ref[1 - i].astype(jnp.float32) + swap_ref[1 - i].astype(jnp.float32)
        part = stay_ref[i] + own_ref[i].astype(jnp.float32) + other
        rows = pl.ds(pl.multiple_of(place_of * half, half), half)
        out_ref[rows, :] = part.astype(out_ref.dtype)


def taken(step, *args):
    return lax.cond(
        lax.axis_index("col") < 16,
        step,
        lambda *a: jax.tree.map(lambda v: jnp.zeros(v.shape, v.dtype), jax.eval_shape(step, *a)),
        *args,
    )


def gather_and_round(gelu_grad, weight):
    line = gather(gelu_grad, along_x[0] + along_y[1])
    weight_other = swap_cores(weight)
    grad_tokens = gather(line, along_y[0] + along_x[1])
    grad_blocks = grad_tokens.reshape((16,) + gelu_grad.shape)

    weights = weight, weight_other
    far, ahead, behind = partials(early_groups, (5, 4), grad_blocks, weights)
    far, later_blocks = lax.optimization_barrier((far, grad_blocks))
    far = send(far, 2)
    own, cross = send(ahead, 1), send(behind, -1, cross=True)
    rest, for_sibling = partials(late_groups, (7,), later_blocks, weights, far)
    rest_other = swap_cores(for_sibling)

    both = (2,) + rest.shape[1:]
    outs = [
        jax.ShapeDtypeStruct((2,) + both, jnp.bfloat16),
        jax.ShapeDtypeStruct(both, jnp.float32),
        jax.ShapeDtypeStruct(both, jnp.float32),
    ]
    return (*call(first_kernel, outs, (own, cross, rest, rest_other)), grad_blocks)


def weight_kernel(sibling, input_ref, grad_ref, *refs):
    first_ref = refs[0] if len(refs) == 3 else None
    out_ref, rows_ref = refs[-2:]
    half, depth = grad_ref.shape[1:]
    core = lax.rem(lax.axis_index("rep"), 2)
    core = 1 - core if sibling else core
    for chip in range(16):
        at = jnp.where(core == 0, (chip % 4) * 4 + chip // 4, chip)
        rows = pl.ds(pl.multiple_of(at * half, half), half)
        rows_ref[rows, :] = input_ref[chip, core]
    tile = 256
    for start in range(0, depth, tile):
        grad = grad_ref[:, :, start : start + tile].reshape(16 * half, tile)
        part = matmul_tn(rows_ref[...], grad)
        if first_ref is not None:
            part = part + first_ref[:, start : start + tile]
        out_ref[:, start : start + tile] = part


def weight_gradient(sibling, input_whole, grad_blocks, *first):
    tokens, width = input_whole.shape
    half, depth = grad_blocks.shape[1:]
    out = jax.ShapeDtypeStruct((width, depth), jnp.float32)
    return call(
        functools.partial(weight_kernel, sibling),
        [out],
        (input_whole.reshape(16, 2, half, width), grad_blocks, *first),
        flops=(1 if sibling else 40) * tokens * width * depth,
        scratch=[pltpu.VMEM((tokens // 2, width), jnp.bfloat16)],
    )[0]


def local(layer_input, weight, gelu_input, upstream):
    tokens, width = layer_input.shape
    half = tokens // 2
    f32, bf16 = jnp.float32, jnp.bfloat16

    input_whole = lax.all_gather(layer_input, "col", axis=0, tiled=True)
    gelu_grad = (upstream.astype(f32) * gelu_slope(gelu_input.astype(f32))).astype(bf16)

    to_send, middle, here, grad_blocks = taken(gather_and_round, gelu_grad, weight)

    moved = send(to_send, 2)
    grad_other = swap_cores(grad_blocks)
    own_weight = weight_gradient(False, input_whole, grad_blocks)
    moved, own_weight = lax.optimization_barrier((moved, own_weight))
    part = (2, half, width)
    outs = [jax.ShapeDtypeStruct(part, t) for t in (bf16, bf16, f32, bf16)]
    own, cross, stay, swapped = call(second_kernel, outs, (moved, middle, here))
    last = send(own, 4), send(cross, 4, cross=True), stay, swap_cores(swapped)
    grad_weight = weight_gradient(True, input_whole, grad_other, own_weight)
    last, grad_weight = lax.optimization_barrier((last, grad_weight))
    outs = [jax.ShapeDtypeStruct((tokens, width), bf16)]
    grad_input = call(third_kernel, outs, last)[0]
    return (grad_input, grad_weight)


def solution(mesh):
    in_specs = (
        P("col", ("row", "rep")),
        P(("row", "rep"), "col"),
        P(("row", "rep"), "col"),
        P(("row", "rep"), "col"),
    )
    out_specs = (P("col", ("row", "rep")), P(("row", "rep"), "col"))
    return jax.shard_map(local, mesh=mesh, in_specs=in_specs, out_specs=out_specs, check_vma=False)
```

```python
import functools
import math

import jax
import jax.numpy as jnp
from jax import lax
from jax.experimental import pallas as pl
from jax.experimental.pallas import tpu as pltpu
from jax.sharding import PartitionSpec as P

cubic_term = 0.044715
plane = ("row", "rep")
ring = ("col", "rep")


def gelu_slope(values):
    scale = math.sqrt(2.0 / math.pi)
    inner = scale * (values + cubic_term * values * values * values)
    tangent = jnp.tanh(inner)
    return 0.5 * (1.0 + tangent) + 0.5 * values * (1.0 - tangent * tangent) * scale * (
        1.0 + 3.0 * cubic_term * values * values
    )


def index(x, y, core):
    return ((x * 2 + y % 2) * 2 + y // 2) * 2 + core


y_order = (0, 2, 1, 3)
along_x = [[[index(x, y, core) for x in range(4)] for y in y_order] for core in range(2)]
along_y = [[[index(x, y, core) for y in y_order] for x in range(4)] for core in range(2)]


early_groups = (((8,), False), ((7, 5, 3, 1), False), ((-7, -5, -3, -1), True))
late_groups = (((6, 4, 2, 0), False), ((-6, -4, -2), True))


def place(chip, core):
    turned = lax.rem(chip, 4) * 4 + lax.div(chip, 4)
    return jnp.where(core == 0, turned, chip)


def gather(values, groups):
    copies = jnp.broadcast_to(values[None], (4,) + values.shape)
    parts = lax.all_to_all(copies, plane, 0, 0, axis_index_groups=groups)
    return parts.reshape((4 * values.shape[0],) + values.shape[1:])


def swap_cores(values):
    return lax.ppermute(values, "rep", [(0, 1), (1, 0), (2, 3), (3, 2)])


def send(values, distance, cross=False):
    pairs = []
    for z in range(16):
        for rep in range(4):
            target = (z + (-distance if rep % 2 else distance)) % 16
            pairs.append((z * 4 + rep, target * 4 + (rep ^ 1 if cross else rep)))
    return lax.ppermute(values, ring, pairs)


def matmul_nt(a, b):
    return lax.dot_general(a, b, (((1,), (1,)), ((), ())), preferred_element_type=jnp.float32)


def matmul_tn(a, b):
    return lax.dot_general(a, b, (((0,), (0,)), ((), ())), preferred_element_type=jnp.float32)


def call(kernel, outs, args, flops=0, scratch=()):
    vmem = pl.BlockSpec(memory_space=pltpu.VMEM)
    moved = sum(v.size * v.dtype.itemsize for v in tuple(args) + tuple(outs))
    return pl.pallas_call(
        kernel,
        out_shape=outs,
        in_specs=[vmem] * len(args),
        out_specs=tuple(vmem for _ in outs),
        scratch_shapes=scratch,
        compiler_params=pltpu.CompilerParams(vmem_limit_bytes=40 * 1024 * 1024),
        cost_estimate=pl.CostEstimate(flops=flops, bytes_accessed=moved, transcendentals=0),
    )(*args)


def partial_kernel(groups, dots, grad_ref, own_ref, other_ref, *refs):
    outs = refs[-len(groups) :]
    add_ref = refs[0] if len(refs) > len(groups) else None
    core = lax.rem(lax.axis_index("rep"), 2)
    z = lax.axis_index("col")
    width = own_ref.shape[0]
    blocks = [
        (out_ref, i, flipped, lax.rem(z + (1 - 2 * core) * step + 16, 16))
        for (steps, flipped), out_ref in zip(groups, outs)
        for i, step in enumerate(steps)
    ]
    start = 0
    for count in dots:
        taken_now = blocks[start : start + count]
        rows = jnp.concatenate([grad_ref[place(chip, core)] for _, _, _, chip in taken_now], axis=0)
        for side, ref in enumerate((own_ref, other_ref)):
            part = matmul_nt(rows, ref[...]).reshape(count, -1, width)
            for j, (out_ref, i, flipped, _) in enumerate(taken_now):
                at = (1 - side if flipped else side) * width
                value = part[j]
                if add_ref is not None and start + j == 0:
                    value = value + add_ref[0, :, at : at + width].astype(jnp.float32)
                out_ref[i, :, at : at + width] = value.astype(out_ref.dtype)
        start += count


def partials(groups, dots, grad_blocks, weights, *add):
    rows, depth = grad_blocks.shape[1:]
    width = weights[0].shape[0]
    return call(
        functools.partial(partial_kernel, groups, dots),
        [jax.ShapeDtypeStruct((len(g[0]), rows, 2 * width), jnp.bfloat16) for g in groups],
        (grad_blocks, *weights, *add),
        flops=12 * sum(dots) * rows * depth * width,
    )


def first_kernel(own_ref, cross_ref, far_ref, rest_ref, other_ref, *outs):
    send_ref, middle_ref, here_ref = outs

    def total(i, *refs):
        return sum(ref[i].astype(jnp.float32) for ref in refs)

    dtype = send_ref.dtype
    send_ref[0, 0] = (total(0, own_ref, rest_ref) + far_ref[0].astype(jnp.float32)).astype(dtype)
    send_ref[0, 1] = total(0, cross_ref, other_ref).astype(dtype)
    send_ref[1, 0] = total(2, own_ref, rest_ref).astype(dtype)
    send_ref[1, 1] = total(2, cross_ref, other_ref).astype(dtype)
    middle_ref[0] = total(1, own_ref, rest_ref)
    middle_ref[1] = total(1, cross_ref, other_ref)
    here_ref[0] = total(3, own_ref, rest_ref)
    here_ref[1] = total(3, cross_ref)


def second_kernel(moved_ref, middle_ref, here_ref, own_ref, cross_ref, stay_ref, swap_ref):
    width = own_ref.shape[2]
    ahead = (middle_ref[...] + moved_ref[0].astype(jnp.float32)).astype(own_ref.dtype)
    own_ref[...] = ahead[:, :, :width]
    cross_ref[...] = ahead[:, :, width:]
    here = here_ref[...] + moved_ref[1].astype(jnp.float32)
    stay_ref[...] = here[:, :, :width]
    swap_ref[...] = here[:, :, width:].astype(swap_ref.dtype)


def third_kernel(own_ref, cross_ref, stay_ref, swap_ref, out_ref):
    half = own_ref.shape[1]
    core = lax.rem(lax.axis_index("rep"), 2)
    for i, place_of in enumerate((core, 1 - core)):
        other = cross_ref[1 - i].astype(jnp.float32) + swap_ref[1 - i].astype(jnp.float32)
        part = stay_ref[i] + own_ref[i].astype(jnp.float32) + other
        rows = pl.ds(pl.multiple_of(place_of * half, half), half)
        out_ref[rows, :] = part.astype(out_ref.dtype)


def taken(step, *args):
    return lax.cond(
        lax.axis_index("col") < 16,
        step,
        lambda *a: jax.tree.map(lambda v: jnp.zeros(v.shape, v.dtype), jax.eval_shape(step, *a)),
        *args,
    )


def gather_and_round(gelu_grad, weight):
    line = gather(gelu_grad, along_x[0] + along_y[1])
    weight_other = swap_cores(weight)
    grad_tokens = gather(line, along_y[0] + along_x[1])
    grad_blocks = grad_tokens.reshape((16,) + gelu_grad.shape)

    weights = weight, weight_other
    far, ahead, behind = partials(early_groups, (5, 4), grad_blocks, weights)
    far, later_blocks = lax.optimization_barrier((far, grad_blocks))
    far = send(far, 2)
    own, cross = send(ahead, 1), send(behind, -1, cross=True)
    rest, for_sibling = partials(late_groups, (7,), later_blocks, weights)
    rest_other = swap_cores(for_sibling)

    both = (2,) + rest.shape[1:]
    outs = [
        jax.ShapeDtypeStruct((2,) + both, jnp.bfloat16),
        jax.ShapeDtypeStruct(both, jnp.float32),
        jax.ShapeDtypeStruct(both, jnp.float32),
    ]
    return (*call(first_kernel, outs, (own, cross, far, rest, rest_other)), grad_blocks)


def weight_kernel(sibling, input_ref, grad_ref, *refs):
    first_ref = refs[0] if len(refs) == 3 else None
    out_ref, rows_ref = refs[-2:]
    half, depth = grad_ref.shape[1:]
    core = lax.rem(lax.axis_index("rep"), 2)
    core = 1 - core if sibling else core
    for chip in range(16):
        at = jnp.where(core == 0, (chip % 4) * 4 + chip // 4, chip)
        rows = pl.ds(pl.multiple_of(at * half, half), half)
        rows_ref[rows, :] = input_ref[chip, core]
    tile = 256
    for start in range(0, depth, tile):
        grad = grad_ref[:, :, start : start + tile].reshape(16 * half, tile)
        part = matmul_tn(rows_ref[...], grad)
        if first_ref is not None:
            part = part + first_ref[:, start : start + tile]
        out_ref[:, start : start + tile] = part


def weight_gradient(sibling, input_whole, grad_blocks, *first):
    tokens, width = input_whole.shape
    half, depth = grad_blocks.shape[1:]
    out = jax.ShapeDtypeStruct((width, depth), jnp.float32)
    return call(
        functools.partial(weight_kernel, sibling),
        [out],
        (input_whole.reshape(16, 2, half, width), grad_blocks, *first),
        flops=(1 if sibling else 40) * tokens * width * depth,
        scratch=[pltpu.VMEM((tokens // 2, width), jnp.bfloat16)],
    )[0]


def local(layer_input, weight, gelu_input, upstream):
    tokens, width = layer_input.shape
    half = tokens // 2
    f32, bf16 = jnp.float32, jnp.bfloat16

    input_whole = lax.all_gather(layer_input, "col", axis=0, tiled=True)
    gelu_grad = (upstream.astype(f32) * gelu_slope(gelu_input.astype(f32))).astype(bf16)

    to_send, middle, here, grad_blocks = taken(gather_and_round, gelu_grad, weight)

    moved = send(to_send, 2)
    grad_other = swap_cores(grad_blocks)
    grad_weight = weight_gradient(False, input_whole, grad_blocks)
    grad_weight = weight_gradient(True, input_whole, grad_other, grad_weight)
    moved, grad_weight = lax.optimization_barrier((moved, grad_weight))
    part = (2, half, width)
    outs = [jax.ShapeDtypeStruct(part, t) for t in (bf16, bf16, f32, bf16)]
    own, cross, stay, swapped = call(second_kernel, outs, (moved, middle, here))
    last = send(own, 4), send(cross, 4, cross=True), stay, swap_cores(swapped)
    outs = [jax.ShapeDtypeStruct((tokens, width), bf16)]
    grad_input = call(third_kernel, outs, last)[0]
    return (grad_input, grad_weight)


def solution(mesh):
    in_specs = (
        P("col", ("row", "rep")),
        P(("row", "rep"), "col"),
        P(("row", "rep"), "col"),
        P(("row", "rep"), "col"),
    )
    out_specs = (P("col", ("row", "rep")), P(("row", "rep"), "col"))
    return jax.shard_map(local, mesh=mesh, in_specs=in_specs, out_specs=out_specs, check_vma=False)
```

```python
import functools
import math

import jax
import jax.numpy as jnp
from jax import lax
from jax.experimental import pallas as pl
from jax.experimental.pallas import tpu as pltpu
from jax.sharding import PartitionSpec as P

cubic_term = 0.044715
plane = ("row", "rep")
ring = ("col", "rep")


def gelu_slope(values):
    scale = math.sqrt(2.0 / math.pi)
    inner = scale * (values + cubic_term * values * values * values)
    tangent = jnp.tanh(inner)
    return 0.5 * (1.0 + tangent) + 0.5 * values * (1.0 - tangent * tangent) * scale * (
        1.0 + 3.0 * cubic_term * values * values
    )


def index(x, y, core):
    return ((x * 2 + y % 2) * 2 + y // 2) * 2 + core


y_order = (0, 2, 1, 3)
along_x = [[[index(x, y, core) for x in range(4)] for y in y_order] for core in range(2)]
along_y = [[[index(x, y, core) for y in y_order] for x in range(4)] for core in range(2)]


early_groups = (((8,), False), ((7, 5, 3, 1), False), ((-7, -5, -3, -1), True))
late_groups = (((6, 4, 2, 0), False), ((-6, -4, -2), True))


def place(chip, core):
    turned = lax.rem(chip, 4) * 4 + lax.div(chip, 4)
    return jnp.where(core == 0, turned, chip)


def copy_kernel(values_ref, out_ref, sems):
    copies = [pltpu.make_async_copy(values_ref, out_ref.at[i], sems.at[i]) for i in range(4)]
    for copy in copies:
        copy.start()
    for copy in copies:
        copy.wait()


def four_copies(values):
    return pl.pallas_call(
        copy_kernel,
        out_shape=jax.ShapeDtypeStruct((4,) + values.shape, values.dtype),
        in_specs=[pl.BlockSpec(memory_space=pltpu.VMEM)],
        out_specs=pl.BlockSpec(memory_space=pl.ANY),
        scratch_shapes=[pltpu.SemaphoreType.DMA((4,))],
    )(values)


def gather(values, groups, copied=False):
    copies = four_copies(values) if copied else jnp.broadcast_to(values[None], (4,) + values.shape)
    parts = lax.all_to_all(copies, plane, 0, 0, axis_index_groups=groups)
    return parts.reshape((4 * values.shape[0],) + values.shape[1:])


def swap_cores(values):
    return lax.ppermute(values, "rep", [(0, 1), (1, 0), (2, 3), (3, 2)])


def send(values, distance, cross=False):
    pairs = []
    for z in range(16):
        for rep in range(4):
            target = (z + (-distance if rep % 2 else distance)) % 16
            pairs.append((z * 4 + rep, target * 4 + (rep ^ 1 if cross else rep)))
    return lax.ppermute(values, ring, pairs)


def matmul_nt(a, b):
    return lax.dot_general(a, b, (((1,), (1,)), ((), ())), preferred_element_type=jnp.float32)


def matmul_tn(a, b):
    return lax.dot_general(a, b, (((0,), (0,)), ((), ())), preferred_element_type=jnp.float32)


def call(kernel, outs, args, flops=0, scratch=()):
    vmem = pl.BlockSpec(memory_space=pltpu.VMEM)
    moved = sum(v.size * v.dtype.itemsize for v in tuple(args) + tuple(outs))
    return pl.pallas_call(
        kernel,
        out_shape=outs,
        in_specs=[vmem] * len(args),
        out_specs=tuple(vmem for _ in outs),
        scratch_shapes=scratch,
        compiler_params=pltpu.CompilerParams(vmem_limit_bytes=40 * 1024 * 1024),
        cost_estimate=pl.CostEstimate(flops=flops, bytes_accessed=moved, transcendentals=0),
    )(*args)


def partial_kernel(groups, dots, grad_ref, own_ref, other_ref, *refs):
    outs = refs[-len(groups) :]
    add_ref = refs[0] if len(refs) > len(groups) else None
    core = lax.rem(lax.axis_index("rep"), 2)
    z = lax.axis_index("col")
    width = own_ref.shape[0]
    blocks = [
        (out_ref, i, flipped, lax.rem(z + (1 - 2 * core) * step + 16, 16))
        for (steps, flipped), out_ref in zip(groups, outs)
        for i, step in enumerate(steps)
    ]
    start = 0
    for count in dots:
        taken_now = blocks[start : start + count]
        rows = jnp.concatenate([grad_ref[place(chip, core)] for _, _, _, chip in taken_now], axis=0)
        for side, ref in enumerate((own_ref, other_ref)):
            part = matmul_nt(rows, ref[...]).reshape(count, -1, width)
            for j, (out_ref, i, flipped, _) in enumerate(taken_now):
                at = (1 - side if flipped else side) * width
                value = part[j]
                if add_ref is not None and start + j == 0:
                    value = value + add_ref[0, :, at : at + width].astype(jnp.float32)
                out_ref[i, :, at : at + width] = value.astype(out_ref.dtype)
        start += count


def partials(groups, dots, grad_blocks, weights, *add):
    rows, depth = grad_blocks.shape[1:]
    width = weights[0].shape[0]
    return call(
        functools.partial(partial_kernel, groups, dots),
        [jax.ShapeDtypeStruct((len(g[0]), rows, 2 * width), jnp.bfloat16) for g in groups],
        (grad_blocks, *weights, *add),
        flops=12 * sum(dots) * rows * depth * width,
    )


def first_kernel(own_ref, cross_ref, rest_ref, other_ref, send_ref, middle_ref, here_ref):
    def total(i, *refs):
        return sum(ref[i].astype(jnp.float32) for ref in refs)

    dtype = send_ref.dtype
    send_ref[0, 0] = total(0, own_ref, rest_ref).astype(dtype)
    send_ref[0, 1] = total(0, cross_ref, other_ref).astype(dtype)
    send_ref[1, 0] = total(2, own_ref, rest_ref).astype(dtype)
    send_ref[1, 1] = total(2, cross_ref, other_ref).astype(dtype)
    middle_ref[0] = total(1, own_ref, rest_ref)
    middle_ref[1] = total(1, cross_ref, other_ref)
    here_ref[0] = total(3, own_ref, rest_ref)
    here_ref[1] = total(3, cross_ref)


def second_kernel(moved_ref, middle_ref, here_ref, own_ref, cross_ref, stay_ref, swap_ref):
    width = own_ref.shape[2]
    ahead = (middle_ref[...] + moved_ref[0].astype(jnp.float32)).astype(own_ref.dtype)
    own_ref[...] = ahead[:, :, :width]
    cross_ref[...] = ahead[:, :, width:]
    here = here_ref[...] + moved_ref[1].astype(jnp.float32)
    stay_ref[...] = here[:, :, :width]
    swap_ref[...] = here[:, :, width:].astype(swap_ref.dtype)


def third_kernel(own_ref, cross_ref, stay_ref, swap_ref, out_ref):
    half = own_ref.shape[1]
    core = lax.rem(lax.axis_index("rep"), 2)
    for i, place_of in enumerate((core, 1 - core)):
        other = cross_ref[1 - i].astype(jnp.float32) + swap_ref[1 - i].astype(jnp.float32)
        part = stay_ref[i] + own_ref[i].astype(jnp.float32) + other
        rows = pl.ds(pl.multiple_of(place_of * half, half), half)
        out_ref[rows, :] = part.astype(out_ref.dtype)


def taken(step, *args):
    return lax.cond(
        lax.axis_index("col") < 16,
        step,
        lambda *a: jax.tree.map(lambda v: jnp.zeros(v.shape, v.dtype), jax.eval_shape(step, *a)),
        *args,
    )


def gather_and_round(gelu_grad, weight):
    line = gather(gelu_grad, along_x[0] + along_y[1])
    weight_other = swap_cores(weight)
    grad_tokens = gather(line, along_y[0] + along_x[1], copied=True)
    grad_blocks = grad_tokens.reshape((16,) + gelu_grad.shape)

    weights = weight, weight_other
    far, ahead, behind = partials(early_groups, (5, 4), grad_blocks, weights)
    far, later_blocks = lax.optimization_barrier((far, grad_blocks))
    far = send(far, 2)
    own, cross = send(ahead, 1), send(behind, -1, cross=True)
    rest, for_sibling = partials(late_groups, (7,), later_blocks, weights, far)
    rest_other = swap_cores(for_sibling)

    both = (2,) + rest.shape[1:]
    outs = [
        jax.ShapeDtypeStruct((2,) + both, jnp.bfloat16),
        jax.ShapeDtypeStruct(both, jnp.float32),
        jax.ShapeDtypeStruct(both, jnp.float32),
    ]
    return (*call(first_kernel, outs, (own, cross, rest, rest_other)), grad_blocks)


def weight_kernel(sibling, input_ref, grad_ref, *refs):
    first_ref = refs[0] if len(refs) == 3 else None
    out_ref, rows_ref = refs[-2:]
    half, depth = grad_ref.shape[1:]
    core = lax.rem(lax.axis_index("rep"), 2)
    core = 1 - core if sibling else core
    for chip in range(16):
        at = jnp.where(core == 0, (chip % 4) * 4 + chip // 4, chip)
        rows = pl.ds(pl.multiple_of(at * half, half), half)
        rows_ref[rows, :] = input_ref[chip, core]
    tile = 256
    for start in range(0, depth, tile):
        grad = grad_ref[:, :, start : start + tile].reshape(16 * half, tile)
        part = matmul_tn(rows_ref[...], grad)
        if first_ref is not None:
            part = part + first_ref[:, start : start + tile]
        out_ref[:, start : start + tile] = part


def weight_gradient(sibling, input_whole, grad_blocks, *first):
    tokens, width = input_whole.shape
    half, depth = grad_blocks.shape[1:]
    out = jax.ShapeDtypeStruct((width, depth), jnp.float32)
    return call(
        functools.partial(weight_kernel, sibling),
        [out],
        (input_whole.reshape(16, 2, half, width), grad_blocks, *first),
        flops=(1 if sibling else 40) * tokens * width * depth,
        scratch=[pltpu.VMEM((tokens // 2, width), jnp.bfloat16)],
    )[0]


def local(layer_input, weight, gelu_input, upstream):
    tokens, width = layer_input.shape
    half = tokens // 2
    f32, bf16 = jnp.float32, jnp.bfloat16

    input_whole = lax.all_gather(layer_input, "col", axis=0, tiled=True)
    gelu_grad = (upstream.astype(f32) * gelu_slope(gelu_input.astype(f32))).astype(bf16)

    to_send, middle, here, grad_blocks = taken(gather_and_round, gelu_grad, weight)

    moved = send(to_send, 2)
    grad_other = swap_cores(grad_blocks)
    grad_weight = weight_gradient(False, input_whole, grad_blocks)
    grad_weight = weight_gradient(True, input_whole, grad_other, grad_weight)
    moved, grad_weight = lax.optimization_barrier((moved, grad_weight))
    part = (2, half, width)
    outs = [jax.ShapeDtypeStruct(part, t) for t in (bf16, bf16, f32, bf16)]
    own, cross, stay, swapped = call(second_kernel, outs, (moved, middle, here))
    last = send(own, 4), send(cross, 4, cross=True), stay, swap_cores(swapped)
    outs = [jax.ShapeDtypeStruct((tokens, width), bf16)]
    grad_input = call(third_kernel, outs, last)[0]
    return (grad_input, grad_weight)


def solution(mesh):
    in_specs = (
        P("col", ("row", "rep")),
        P(("row", "rep"), "col"),
        P(("row", "rep"), "col"),
        P(("row", "rep"), "col"),
    )
    out_specs = (P("col", ("row", "rep")), P(("row", "rep"), "col"))
    return jax.shard_map(local, mesh=mesh, in_specs=in_specs, out_specs=out_specs, check_vma=False)
```
